32 devices in a mesh: seq: 16 (over z, y, core), head: 2 (over x).
Axes of the slice: x: 2, y: 2, z: 4, core: 2. Of those that a mesh axis runs over, the one named last changes fastest.
Arguments:
- queries: bfloat16 [16384, 4096], P('seq', 'head'), may hold values from -6 to 6
- keys: bfloat16 [16384, 4096], P('seq', 'head'), may hold values from -6 to 6
- values: bfloat16 [16384, 4096], P('seq', 'head'), may hold values from -6 to 6
- out_weight: bfloat16 [4096, 4096], P('head'), may hold values from -1.5 to 1.5
Outputs:
- mixed: bfloat16 [16384, 4096], P('seq', 'head')
The draws below stay inside these ranges and needn't reach their ends.
All inputs are finite; a program needn't handle non-finite values.
Results may differ from the reference program's by a relative error of at most 0.015.
Values may be sent and summed in bfloat16 or wider, within the bound.
No kernel may reach another device: no remote copies, remote signals or barrier semaphores. Data moves between devices by JAX's collectives and lax.ppermute only.
A program may use at most 192 MiB of HBM per device.

```python
import math
import jax
import jax.numpy as jnp
from jax import lax

HEADS = 32
HEAD_DIM = 128
D = 4096
TOKENS = 16384
SEG1 = 2048
SEG2 = 8192
N_HEAD = 2


def draw_queries(key, part):
    drawn = 1.5 * jnp.clip(jax.random.normal(jax.random.fold_in(key, 11), (TOKENS, D), jnp.float32), -4.0, 4.0)
    return drawn.astype(jnp.bfloat16)


def draw_keys(key, part):
    drawn = jnp.clip(jax.random.normal(jax.random.fold_in(key, 12), (TOKENS, D), jnp.float32), -6.0, 6.0)
    return drawn.astype(jnp.bfloat16)


def block_scale(own_key, shape, shards, smallest, top_value):
    level = 1.0
    for dim, shards_of in shards:
        draws = jax.random.uniform(jax.random.fold_in(jax.random.fold_in(own_key, 6), dim), (shards_of,), jnp.float32, smallest / len(shards), top_value / len(shards))
        level = level * jnp.repeat(jnp.exp(draws), shape[dim] // shards_of).reshape((-1,) + (1,) * (len(shape) - 1 - dim))
    return level


def gaussian(key, shape, scale, limit, split=(), kind=jnp.bfloat16):
    entries = jax.random.normal(key, shape, jnp.float32) * scale
    if len(split) > 0:
        entries = block_scale(key, shape, split, -0.22, 0.18) * entries
    return jnp.clip(entries, min=-limit, max=limit).astype(kind)


def setup_inputs(seed: int = 0) -> dict:
    splits = jax.random.split(jax.random.key(seed), 5)
    queries = draw_queries(jax.random.fold_in(splits[4], 71), 0)
    keys = draw_keys(jax.random.fold_in(splits[4], 71), 0)
    values = gaussian(splits[2], (TOKENS, D), 1.0, 6.0, ((0, 16), (1, 2)))
    out_weight = gaussian(splits[3], (D, D), 0.25, 1.5, ((0, 2),))
    return {"queries": queries, "keys": keys, "values": values, "out_weight": out_weight}


NEG_FILL = -1e+30

def causal_level(query, key_rows, value_rows, seg_len, scale):
    count = query.shape[0] // seg_len
    lower = jnp.arange(seg_len)[:, None] >= jnp.arange(seg_len)[None, :]

    def one_segment(parts):
        seg_query, seg_keys, seg_values = parts
        scores = jnp.dot(seg_query, seg_keys.T, preferred_element_type=jnp.float32) * scale
        scores = jnp.where(lower, scores, NEG_FILL)
        peak = lax.optimization_barrier(jnp.max(scores, axis=1))
        weights = jnp.where(lower, jnp.exp(scores - peak[:, None]), 0.0)
        total = lax.optimization_barrier(jnp.sum(weights, axis=1))
        numer = jnp.dot(weights.astype(jnp.bfloat16), seg_values, preferred_element_type=jnp.float32)
        return (numer, peak, total)
    numer, peak, total = lax.map(one_segment, (query.reshape(count, seg_len, -1), key_rows.reshape(count, seg_len, -1), value_rows.reshape(count, seg_len, -1)))
    return (numer.reshape(-1, numer.shape[-1]), peak.reshape(-1), total.reshape(-1))

def dilated(source, stride, offset):
    shaped = source.reshape(-1, stride, source.shape[1])
    return lax.dynamic_index_in_dim(shaped, offset, axis=1, keepdims=False)

def spread_level(state, stride, offset):
    numer, peak, total = state
    picker = jnp.arange(stride, dtype=jnp.int32) == offset
    numer_full = jnp.where(picker[None, :, None], numer[:, None, :], 0.0).reshape(-1, numer.shape[-1])
    peak_full = jnp.where(picker[None, :], peak[:, None], NEG_FILL).reshape(-1)
    total_full = jnp.where(picker[None, :], total[:, None], 0.0).reshape(-1)
    return (numer_full, peak_full, total_full)

def reference(queries, keys, values, out_weight):
    scale = 1.0 / math.sqrt(HEAD_DIM)

    def one_head(head_id):
        column = head_id * HEAD_DIM
        head_query = lax.dynamic_slice_in_dim(queries, column, HEAD_DIM, 1)
        head_keys = lax.dynamic_slice_in_dim(keys, column, HEAD_DIM, 1)
        head_values = lax.dynamic_slice_in_dim(values, column, HEAD_DIM, 1)
        near = causal_level(head_query, head_keys, head_values, SEG1, scale)
        mid_off = head_id % 4
        middle = causal_level(dilated(head_query, 4, mid_off), dilated(head_keys, 4, mid_off), dilated(head_values, 4, mid_off), SEG2 // 4, scale)
        middle = spread_level(middle, 4, mid_off)
        far_off = head_id % 16
        far = causal_level(dilated(head_query, 16, far_off), dilated(head_keys, 16, far_off), dilated(head_values, 16, far_off), TOKENS // 16, scale)
        far = spread_level(far, 16, far_off)
        top = jnp.maximum(jnp.maximum(near[1], middle[1]), far[1])
        numer = jnp.zeros_like(near[0])
        total = jnp.zeros_like(near[2])
        for level in (near, middle, far):
            factor = jnp.exp(level[1] - top)
            numer = numer + level[0] * factor[:, None]
            total = total + level[2] * factor
        return (numer / total[:, None]).astype(jnp.bfloat16)
    heads_out = lax.map(one_head, jnp.arange(HEADS, dtype=jnp.int32))
    attended = jnp.transpose(heads_out, (1, 0, 2)).reshape(TOKENS, D)
    group_cols = D // N_HEAD
    summed = jnp.zeros((TOKENS, D), jnp.float32)
    for group in range(N_HEAD):
        partial_sum = jnp.dot(attended[:, group * group_cols:(group + 1) * group_cols], out_weight[group * group_cols:(group + 1) * group_cols, :], preferred_element_type=jnp.float32)
        rounded = lax.optimization_barrier(partial_sum.astype(jnp.bfloat16))
        summed = summed + rounded.astype(jnp.float32)
    return summed.astype(jnp.bfloat16)
```

```python
import functools
import math

import jax
import jax.numpy as jnp
from jax import lax
from jax.experimental import pallas as pl
from jax.experimental.pallas import tpu as pltpu
from jax.sharding import PartitionSpec as P

HEAD_DIM = 128
SEG1 = 2048
SEG2 = 8192


NEG_FILL = -1e30
LOG2_SCALE = math.log2(math.e) / math.sqrt(HEAD_DIM)
CHUNK = 256
GROUP = 8
MID_ROWS = CHUNK // 4
FAR_ROWS = CHUNK // 16
STAT_ROWS = 16
VMEM_BYTES = 50 * 2**20
F32 = jnp.float32
BF16 = jnp.bfloat16


def iota(shape, dim):
    return lax.broadcasted_iota(jnp.int32, shape, dim)


def token_of_row(row):
    return 16 * (row & 15) + 4 * ((row >> 4) & 3) + (row >> 6)


def mid_of_row(row):
    return (row >> 6) * 64 + 4 * (row & 15) + ((row >> 4) & 3)


def dot(lhs, rhs):
    return lax.dot_general(lhs, rhs, (((1,), (0,)), ((), ())), preferred_element_type=F32)


def dot_t(lhs, rhs):
    return lax.dot_general(lhs, rhs, (((1,), (1,)), ((), ())), preferred_element_type=F32)


def with_ones(values):
    return jnp.concatenate([values, jnp.ones_like(values)], axis=1)


def attend(query, parts):
    scores = []
    peak = None
    for keys, _, mask in parts:
        score = dot_t(query, keys)
        if mask is not None:
            score = jnp.where(mask, score, NEG_FILL)
        scores.append(score)
        top = jnp.max(score, axis=1, keepdims=True)
        peak = top if peak is None else jnp.maximum(peak, top)
    acc = None
    for score, (_, values, _) in zip(scores, parts):
        weights = jnp.exp2((score - peak) * LOG2_SCALE).astype(BF16)
        term = dot(weights, values)
        acc = term if acc is None else acc + term
    total = acc[:, HEAD_DIM:]
    return acc[:, :HEAD_DIM] / total, peak * LOG2_SCALE + jnp.log2(total)


def merge(out_a, lse_a, out_b, lse_b):
    top = jnp.maximum(lse_a, lse_b)
    fac_a = jnp.exp2(lse_a - top)
    fac_b = jnp.exp2(lse_b - top)
    total = fac_a + fac_b
    return (out_a * fac_a + out_b * fac_b) / total, top + jnp.log2(total)


def prep_kv_kernel(place, k_ref, v_ref, *outs):
    me = place[0]
    for d in range(GROUP):
        owner = me ^ d
        for e in range(2):
            residue = 2 * (owner & 1) + e
            row = iota((MID_ROWS, CHUNK), 0)
            token = 16 * (row & 15) + 4 * (row >> 4) + residue
            pick = (token == iota((MID_ROWS, CHUNK), 1)).astype(F32).astype(BF16)
            column = pl.multiple_of(owner * 256 + e * 128, 128)
            for a, source in enumerate((k_ref, v_ref)):
                outs[d][a, :, e * 128 : (e + 1) * 128] = dot(pick, source[:, pl.ds(column, 128)]).astype(BF16)
        start = pl.multiple_of(((owner >> 1) & 3) * FAR_ROWS, FAR_ROWS)
        for a in range(2):
            outs[GROUP + d][a] = outs[d][a, pl.ds(start, FAR_ROWS), :]


def prep_q_kernel(place, q_ref, rows_ref, *outs):
    me = place[0]
    row = iota((CHUNK, CHUNK), 0)
    pick = (token_of_row(row) == iota((CHUNK, CHUNK), 1)).astype(F32).astype(BF16)
    rows_ref[...] = dot(pick, q_ref[...]).astype(BF16)
    for d in range(GROUP):
        owner = me ^ d
        for e in range(2):
            start = pl.multiple_of((2 * (owner & 1) + e) * MID_ROWS, MID_ROWS)
            column = pl.multiple_of(owner * 256 + e * 128, 128)
            outs[d][:, e * 128 : (e + 1) * 128] = rows_ref[pl.ds(start, MID_ROWS), pl.ds(column, 128)]


def put_lane(ref, rows, lane, value):
    ref[rows, :] = jnp.where(iota((CHUNK, 128), 1) == lane, value, ref[rows, :])


def get_lane(block, lane):
    return jnp.sum(jnp.where(iota(block.shape, 1) == lane, block, 0.0), axis=1, keepdims=True)


def near_own_kernel(chunks, q_ref, k_ref, v_ref, o_ref, lse_ref):
    head = pl.program_id(0)

    @pl.when(head == 0)
    def _():
        lse_ref[...] = jnp.zeros_like(lse_ref)

    mask = token_of_row(iota((CHUNK, CHUNK), 0)) >= iota((CHUNK, CHUNK), 1)
    values = with_ones(v_ref[...])
    for c in range(chunks):
        here = slice(c * CHUNK, (c + 1) * CHUNK)
        parts = [(k_ref[here, :], values[here], mask)]
        if c:
            parts.append((k_ref[: c * CHUNK, :], values[: c * CHUNK], None))
        out, lse = attend(q_ref[here, :], parts)
        o_ref[here, :] = out.astype(BF16)
        put_lane(lse_ref, here, head, lse)


def near_prev_kernel(chunks, place, q_ref, k_ref, v_ref, own_o, own_lse, o_ref, lse_ref):
    head = pl.program_id(0)
    second = (place[0] & 1) == 1

    @pl.when(head == 0)
    def _():
        lse_ref[...] = own_lse[...]

    @pl.when(jnp.logical_not(second))
    def _():
        o_ref[...] = own_o[...]

    @pl.when(second)
    def _():
        values = with_ones(v_ref[...])
        keys = k_ref[...]
        for c in range(chunks):
            here = slice(c * CHUNK, (c + 1) * CHUNK)
            out, lse = attend(q_ref[here, :], [(keys, values, None)])
            out, lse = merge(
                out, lse, own_o[here, :].astype(F32), get_lane(own_lse[here, :], head)
            )
            o_ref[here, :] = out.astype(BF16)
            put_lane(lse_ref, here, head, lse)


def mid_kernel(rows, place, *refs):
    kv_in, q_in, far_in = refs[:GROUP], refs[GROUP : 2 * GROUP], refs[2 * GROUP : 3 * GROUP]
    outs = refs[3 * GROUP : 4 * GROUP]
    kv, q, far_kv, res, lses, sems = refs[4 * GROUP :]
    me = place[0]
    later = place[1]
    copies = []
    for d in range(GROUP):
        owner = me ^ d
        copies.append(pltpu.make_async_copy(kv_in[d], kv.at[owner], sems.at[d]))
        copies.append(pltpu.make_async_copy(q_in[d], q.at[owner], sems.at[GROUP + d]))
        copies.append(pltpu.make_async_copy(far_in[d], far_kv.at[owner], sems.at[2 * GROUP + d]))
    for copy in copies:
        copy.start()
    for copy in copies:
        copy.wait()
    mask = mid_of_row(iota((rows, rows), 0)) >= mid_of_row(iota((rows, rows), 1))
    for e in range(2):
        lanes = slice(e * 128, (e + 1) * 128)
        for i in range(GROUP):
            parts = [(kv[i, 0, :, lanes], with_ones(kv[i, 1, :, lanes]), mask)]
            if i:
                parts.append(
                    (
                        kv[:i, 0, :, lanes].reshape(i * rows, 128),
                        with_ones(kv[:i, 1, :, lanes].reshape(i * rows, 128)),
                        None,
                    )
                )
            out, lse = attend(q[i, :, lanes], parts)
            res[e, i] = out
            lses[e, i] = lse
    start = pl.multiple_of(((me >> 1) & 3) * FAR_ROWS, FAR_ROWS)
    chunks = rows // MID_ROWS
    count = GROUP * chunks * FAR_ROWS
    mask = iota((count, count), 0) >= iota((count, count), 1)
    for e in range(2):
        lanes = slice(e * 128, (e + 1) * 128)

        def dilated(pick):
            pieces = []
            for i in range(GROUP):
                for c in range(chunks):
                    pieces.append(pick(i, pl.ds(start + c * MID_ROWS, FAR_ROWS)))
            return jnp.concatenate(pieces, axis=0)

        query = dilated(lambda i, at: q[i, at, lanes])
        keys = dilated(lambda i, at: kv[i, 0, at, lanes])
        values = dilated(lambda i, at: kv[i, 1, at, lanes])
        other_keys = far_kv[:, 0, :, lanes].reshape(count, 128)
        other_values = far_kv[:, 1, :, lanes].reshape(count, 128)
        out, lse = attend(
            query,
            [
                (keys, with_ones(values), mask),
                (other_keys, with_ones(other_values), jnp.broadcast_to(later == 1, (count, count))),
            ],
        )
        for i in range(GROUP):
            for c in range(chunks):
                at = pl.ds(start + c * MID_ROWS, FAR_ROWS)
                piece = slice((i * chunks + c) * FAR_ROWS, (i * chunks + c + 1) * FAR_ROWS)
                res[e, i, at, :], lses[e, i, at, :] = merge(
                    res[e, i, at, :], lses[e, i, at, :], out[piece], lse[piece]
                )
    lane = iota((rows, 128), 1)
    stats = jnp.zeros((rows, 128), F32)
    for d in range(GROUP):
        for e in range(2):
            stats = jnp.where(lane == 8 * d + e, lses[e, me ^ d], stats)
    stats = jnp.transpose(stats)
    high = stats.astype(BF16).astype(F32)
    low = stats - high
    for d in range(GROUP):
        for e in range(2):
            outs[d][:rows, e * 128 : (e + 1) * 128] = res[e, me ^ d].astype(BF16)
        outs[d][rows:, :] = jnp.concatenate(
            [high[8 * d : 8 * d + 8], low[8 * d : 8 * d + 8]], axis=0
        ).astype(BF16)


def combine_kernel(rows, chunk, place, o_ref, lse_ref, *refs):
    back = refs[:GROUP]
    w_ref, send_ref, att_ref, work = refs[GROUP:]

    @pl.when(pl.program_id(0) == 0)
    def _():
        me = place[0]
        work[...] = o_ref[...]
        stats = []
        for d in range(GROUP):
            tile = back[d][rows:, :].astype(F32)
            stats.append(tile[:8] + tile[8:])
        stats.append(jnp.zeros((128 - 8 * GROUP, rows), F32))
        stats = jnp.transpose(jnp.concatenate(stats, axis=0))
        stats = stats[chunk * MID_ROWS : (chunk + 1) * MID_ROWS]
        for d in range(GROUP):
            owner = me ^ d
            for e in range(2):
                start = pl.multiple_of((2 * (owner & 1) + e) * MID_ROWS, MID_ROWS)
                column = pl.multiple_of(owner * 256 + e * 128, 128)
                at = (pl.ds(start, MID_ROWS), pl.ds(column, 128))
                near = o_ref[at].astype(F32)
                near_lse = get_lane(lse_ref[pl.ds(start, MID_ROWS), :], 2 * owner + e)
                mid = back[d][chunk * MID_ROWS : (chunk + 1) * MID_ROWS, e * 128 : (e + 1) * 128]
                mid_lse = stats[:, 8 * d + e : 8 * d + e + 1]
                out, _ = merge(near, near_lse, mid.astype(F32), mid_lse)
                work[at] = out.astype(BF16)
        row = token_of_row(iota((CHUNK, CHUNK), 1))
        pick = (row == iota((CHUNK, CHUNK), 0)).astype(F32).astype(BF16)
        att_ref[...] = dot(pick, work[...]).astype(BF16)

    send_ref[...] = dot(att_ref[...], w_ref[...]).astype(BF16)


def project_kernel(place, att_ref, w_ref, out_ref):
    out_ref[...] = dot(att_ref[...], w_ref[...]).astype(BF16)


def params():
    return pltpu.CompilerParams(vmem_limit_bytes=VMEM_BYTES)


def fast_shards(queries, keys, values, out_weight):
    tokens, width = queries.shape
    heads = width // HEAD_DIM
    features = out_weight.shape[1]
    chunks = tokens // CHUNK
    mid_rows = tokens // 4
    far_rows = tokens // 16
    seq_index = lax.axis_index("seq")
    head_index = lax.axis_index("head")
    place = jnp.stack([seq_index % GROUP, seq_index // GROUP, head_index]).astype(jnp.int32)
    shape = jax.ShapeDtypeStruct

    def spec(block, index):
        return pl.BlockSpec(block, index)

    seq_size = lax.axis_size("seq")
    swaps = [[(i, i ^ d) for i in range(seq_size)] for d in range(GROUP)]
    ahead = [[(i, (i ^ d) + GROUP) for i in range(seq_size - GROUP)] for d in range(GROUP)]

    prev_k = lax.ppermute(keys, "seq", [(i, i + 1) for i in range(0, seq_size, 2)])
    prev_v = lax.ppermute(values, "seq", [(i, i + 1) for i in range(0, seq_size, 2)])

    blocks = pl.pallas_call(
        prep_kv_kernel,
        grid_spec=pltpu.PrefetchScalarGridSpec(
            num_scalar_prefetch=1,
            grid=(chunks,),
            in_specs=[spec((CHUNK, width), lambda c, p: (c, 0))] * 2,
            out_specs=[spec((2, MID_ROWS, 256), lambda c, p: (0, c, 0))] * GROUP
            + [spec((2, FAR_ROWS, 256), lambda c, p: (0, c, 0))] * GROUP,
        ),
        out_shape=[shape((2, mid_rows, 256), BF16)] * GROUP + [shape((2, far_rows, 256), BF16)] * GROUP,
        compiler_params=params(),
        name="prep_kv",
    )(place, keys, values)
    kv_blocks, far_blocks = blocks[:GROUP], blocks[GROUP:]
    kv_in = [kv_blocks[0]] + [lax.ppermute(kv_blocks[d], "seq", swaps[d]) for d in range(1, GROUP)]
    far_in = [lax.ppermute(far_blocks[d], "seq", ahead[d]) for d in range(GROUP)]

    ordered, *q_blocks = pl.pallas_call(
        prep_q_kernel,
        grid_spec=pltpu.PrefetchScalarGridSpec(
            num_scalar_prefetch=1,
            grid=(chunks,),
            in_specs=[spec((CHUNK, width), lambda c, p: (c, 0))],
            out_specs=[spec((CHUNK, width), lambda c, p: (c, 0))]
            + [spec((MID_ROWS, 256), lambda c, p: (c, 0))] * GROUP,
        ),
        out_shape=[shape((tokens, width), BF16)] + [shape((mid_rows, 256), BF16)] * GROUP,
        compiler_params=params(),
        name="prep_q",
    )(place, queries)
    q_in = [q_blocks[0]] + [lax.ppermute(q_blocks[d], "seq", swaps[d]) for d in range(1, GROUP)]

    column = spec((tokens, HEAD_DIM), lambda h, *_: (0, h))
    whole_lse = spec((tokens, 128), lambda h, *_: (0, 0))
    near_o, near_lse = pl.pallas_call(
        functools.partial(near_own_kernel, chunks),
        grid=(heads,),
        in_specs=[column] * 3,
        out_specs=[column, whole_lse],
        out_shape=[shape((tokens, width), BF16), shape((tokens, 128), F32)],
        compiler_params=params(),
        cost_estimate=pl.CostEstimate(
            flops=heads * 4 * tokens * tokens // 2 * HEAD_DIM, bytes_accessed=4 * tokens * width * 2, transcendentals=0
        ),
        name="near_own",
    )(ordered, keys, values)
    near_o, near_lse = pl.pallas_call(
        functools.partial(near_prev_kernel, chunks),
        grid_spec=pltpu.PrefetchScalarGridSpec(
            num_scalar_prefetch=1,
            grid=(heads,),
            in_specs=[column] * 4 + [whole_lse],
            out_specs=[column, whole_lse],
        ),
        out_shape=[shape((tokens, width), BF16), shape((tokens, 128), F32)],
        compiler_params=params(),
        cost_estimate=pl.CostEstimate(
            flops=heads * 4 * tokens * tokens * HEAD_DIM, bytes_accessed=4 * tokens * width * 2, transcendentals=0
        ),
        name="near_prev",
    )(place, ordered, prev_k, prev_v, near_o, near_lse)

    anywhere = pl.BlockSpec(memory_space=pl.ANY)
    back_rows = mid_rows + STAT_ROWS
    back = pl.pallas_call(
        functools.partial(mid_kernel, mid_rows),
        grid_spec=pltpu.PrefetchScalarGridSpec(
            num_scalar_prefetch=1,
            grid=(1,),
            in_specs=[anywhere] * (3 * GROUP),
            out_specs=[spec((back_rows, 256), lambda s, p: (0, 0))] * GROUP,
            scratch_shapes=[
                pltpu.VMEM((GROUP, 2, mid_rows, 256), BF16),
                pltpu.VMEM((GROUP, mid_rows, 256), BF16),
                pltpu.VMEM((GROUP, 2, far_rows, 256), BF16),
                pltpu.VMEM((2, GROUP, mid_rows, 128), F32),
                pltpu.VMEM((2, GROUP, mid_rows, 128), F32),
                pltpu.SemaphoreType.DMA((3 * GROUP,)),
            ],
        ),
        out_shape=[shape((back_rows, 256), BF16)] * GROUP,
        compiler_params=params(),
        cost_estimate=pl.CostEstimate(
            flops=2 * 4 * (GROUP * mid_rows) ** 2 // 2 * HEAD_DIM, bytes_accessed=4 * 2**20, transcendentals=0
        ),
        name="mid",
    )(place, *kv_in, *q_in, *far_in)
    returned = [back[0]] + [lax.ppermute(back[d], "seq", swaps[d]) for d in range(1, GROUP)]

    half = features // 2
    tile = 512
    tiles = half // tile
    received = []
    attended = []
    for c in range(chunks):
        send, att = pl.pallas_call(
            functools.partial(combine_kernel, mid_rows, c),
            grid_spec=pltpu.PrefetchScalarGridSpec(
                num_scalar_prefetch=1,
                grid=(tiles,),
                in_specs=[
                    spec((CHUNK, width), lambda n, p, c=c: (c, 0)),
                    spec((CHUNK, 128), lambda n, p, c=c: (c, 0)),
                ]
                + [spec((back_rows, 256), lambda n, p: (0, 0))] * GROUP
                + [spec((width, tile), lambda n, p: (0, (1 - p[2]) * tiles + n))],
                out_specs=[
                    spec((CHUNK, tile), lambda n, p: (0, n)),
                    spec((CHUNK, width), lambda n, p: (0, 0)),
                ],
                scratch_shapes=[pltpu.VMEM((CHUNK, width), BF16)],
            ),
            out_shape=[shape((CHUNK, half), BF16), shape((CHUNK, width), BF16)],
            compiler_params=params(),
            cost_estimate=pl.CostEstimate(
                flops=2 * CHUNK * width * half, bytes_accessed=width * half * 2, transcendentals=0
            ),
            name="combine",
        )(place, near_o, near_lse, *returned, out_weight)
        received.append(lax.ppermute(send, "head", [(0, 1), (1, 0)]))
        attended.append(att)
    mixed = []
    for c in range(chunks):
        own = pl.pallas_call(
            project_kernel,
            grid_spec=pltpu.PrefetchScalarGridSpec(
                num_scalar_prefetch=1,
                grid=(tiles,),
                in_specs=[
                    spec((CHUNK, width), lambda n, p: (0, 0)),
                    spec((width, tile), lambda n, p: (0, p[2] * tiles + n)),
                ],
                out_specs=spec((CHUNK, tile), lambda n, p: (0, n)),
            ),
            out_shape=shape((CHUNK, half), BF16),
            compiler_params=params(),
            cost_estimate=pl.CostEstimate(
                flops=2 * CHUNK * width * half, bytes_accessed=width * half * 2, transcendentals=0
            ),
            name="project",
        )(place, attended[c], out_weight)
        mixed.append((own.astype(F32) + received[c].astype(F32)).astype(BF16))
    return jnp.concatenate(mixed, axis=0)


def fits_fast(mesh, queries):
    seq, head = mesh.shape["seq"], mesh.shape["head"]
    tokens = queries.shape[0] // seq
    heads = queries.shape[1] // HEAD_DIM // head
    return (
        head == 2
        and heads == 2 * GROUP
        and seq == 2 * GROUP
        and tokens % CHUNK == 0
        and SEG1 == 2 * tokens
        and SEG2 == GROUP * tokens
    )


def passed_along(value, axis, steps):
    count = lax.axis_size(axis)
    leading, last = (max(0, -steps), min(count, count - steps))
    return lax.ppermute(value, axis, [(source, source + steps) for source in range(leading, last)])


def attend_block(query, key_rows, value_rows, valid, scale):
    scores = jnp.einsum("qhd,khd->hqk", query, key_rows, preferred_element_type=jnp.float32) * scale
    scores = jnp.where(valid, scores, NEG_FILL)
    peak = jnp.max(scores, axis=-1)
    weights = jnp.where(valid, jnp.exp(scores - peak[..., None]), 0.0)
    total = jnp.sum(weights, axis=-1)
    numer = jnp.einsum(
        "hqk,khd->hqd", weights.astype(jnp.bfloat16), value_rows, preferred_element_type=jnp.float32
    )
    return (numer, peak, total)


def absorb_block(state, query, key_rows, value_rows, valid, scale):
    numer, peak, total = state
    scores = jnp.einsum("qhd,khd->hqk", query, key_rows, preferred_element_type=jnp.float32) * scale
    scores = jnp.where(valid, scores, NEG_FILL)
    new_peak = jnp.maximum(peak, jnp.max(scores, axis=-1))
    weights = jnp.where(valid, jnp.exp(scores - new_peak[..., None]), 0.0)
    added = jnp.einsum(
        "hqk,khd->hqd", weights.astype(jnp.bfloat16), value_rows, preferred_element_type=jnp.float32
    )
    return (added, new_peak, jnp.sum(weights, axis=-1))


def take_dilated(source, stride, offsets):
    count = source.shape[0] // stride
    shaped = source.reshape(count, stride, offsets.shape[0], -1)
    picker = (jnp.arange(stride)[:, None] == offsets[None, :]).astype(source.dtype)
    return jnp.sum(shaped * picker[None, :, :, None], axis=1).reshape(count, -1)


def spread_rows(state, stride, offsets):
    numer, peak, total = state
    heads_here, count = peak.shape
    picker = jnp.arange(stride)[None, :] == offsets[:, None]
    numer_full = jnp.where(picker[:, None, :, None], numer[:, :, None, :], 0.0).reshape(
        heads_here, count * stride, -1
    )
    peak_full = jnp.where(picker[:, None, :], peak[:, :, None], NEG_FILL).reshape(
        heads_here, count * stride
    )
    total_full = jnp.where(picker[:, None, :], total[:, :, None], 0.0).reshape(
        heads_here, count * stride
    )
    return (numer_full, peak_full, total_full)


def shards(queries, keys, values, out_weight):
    tok_rows = queries.shape[0]
    heads_here = queries.shape[1] // HEAD_DIM
    scale = 1.0 / math.sqrt(HEAD_DIM)
    seq_index = lax.axis_index("seq")
    head_index = lax.axis_index("head")
    head_ids = head_index * heads_here + jnp.arange(heads_here)
    query_pos = seq_index * tok_rows + jnp.arange(tok_rows)
    near_span = SEG1 // tok_rows
    near_keys, near_values = (keys, values)
    level_bit = 0
    moved = passed_along((near_keys, near_values), "seq", 1 << level_bit)
    near_keys = jnp.concatenate([moved[0], near_keys], axis=0)
    near_values = jnp.concatenate([moved[1], near_values], axis=0)
    near_pos = (seq_index - near_span + 1) * tok_rows + jnp.arange(near_span * tok_rows)
    near_start = seq_index // near_span * near_span * tok_rows
    near_valid = (near_pos[None, :] <= query_pos[:, None]) & (near_pos[None, :] >= near_start)

    def near_head(head_slot):
        column = head_slot * HEAD_DIM
        query = lax.dynamic_slice_in_dim(queries, column, HEAD_DIM, 1)[:, None, :]
        key_rows = lax.dynamic_slice_in_dim(near_keys, column, HEAD_DIM, 1)[:, None, :]
        value_rows = lax.dynamic_slice_in_dim(near_values, column, HEAD_DIM, 1)[:, None, :]
        numer, peak, total = attend_block(query, key_rows, value_rows, near_valid[None], scale)
        return (numer[0], peak[0], total[0])

    near_state = lax.map(near_head, jnp.arange(heads_here))
    mid_offsets = head_ids % 4
    far_offsets = head_ids % 16
    mid_count = tok_rows // 4
    far_count = tok_rows // 16
    mid_query = take_dilated(queries, 4, mid_offsets).reshape(mid_count, heads_here, HEAD_DIM)
    far_query = take_dilated(queries, 16, far_offsets).reshape(far_count, heads_here, HEAD_DIM)
    mid_keys = take_dilated(keys, 4, mid_offsets)
    mid_values = take_dilated(values, 4, mid_offsets)
    mid_qpos = seq_index * tok_rows + mid_offsets[:, None] + 4 * jnp.arange(mid_count)[None, :]
    far_qpos = seq_index * tok_rows + far_offsets[:, None] + 16 * jnp.arange(far_count)[None, :]
    mid_span = SEG2 // tok_rows
    mid_start = seq_index // mid_span * mid_span * tok_rows
    empty_far = (
        jnp.zeros((heads_here, far_count, HEAD_DIM), jnp.float32),
        jnp.full((heads_here, far_count), NEG_FILL, jnp.float32),
        jnp.zeros((heads_here, far_count), jnp.float32),
    )
    block_keys, block_values = (mid_keys, mid_values)
    for level_bit in range(mid_span.bit_length() - 1):
        moved = passed_along((block_keys, block_values), "seq", 1 << level_bit)
        block_keys = jnp.concatenate([moved[0], block_keys], axis=0)
        block_values = jnp.concatenate([moved[1], block_values], axis=0)
    key_index = jnp.arange(mid_span * mid_count)
    mid_kpos = (
        (seq_index - mid_span + 1) * tok_rows
        + (key_index // mid_count * tok_rows + 4 * (key_index % mid_count))[None, :]
        + mid_offsets[:, None]
    )
    mid_valid = (mid_kpos[:, None, :] <= mid_qpos[:, :, None]) & (mid_kpos[:, None, :] >= mid_start)
    mid_state = attend_block(
        mid_query,
        block_keys.reshape(-1, heads_here, HEAD_DIM),
        block_values.reshape(-1, heads_here, HEAD_DIM),
        mid_valid,
        scale,
    )
    far_keys = take_dilated(keys, 16, far_offsets)
    far_values = take_dilated(values, 16, far_offsets)
    piece = (
        lax.all_gather(far_keys, "seq", axis=0, tiled=True),
        lax.all_gather(far_values, "seq", axis=0, tiled=True),
    )
    count = piece[0].shape[0]
    row_index = jnp.arange(count)
    key_pos = (row_index // far_count * tok_rows + 16 * (row_index % far_count))[
        None, :
    ] + far_offsets[:, None]
    valid = key_pos[:, None, :] <= far_qpos[:, :, None]
    far_state = absorb_block(
        empty_far,
        far_query,
        piece[0].reshape(count, heads_here, HEAD_DIM),
        piece[1].reshape(count, heads_here, HEAD_DIM),
        valid,
        scale,
    )
    levels = (
        near_state,
        spread_rows(mid_state, 4, mid_offsets),
        spread_rows(far_state, 16, far_offsets),
    )
    top = jnp.maximum(jnp.maximum(levels[0][1], levels[1][1]), levels[2][1])
    numer = jnp.zeros_like(levels[0][0])
    total = jnp.zeros_like(levels[0][2])
    for level in levels:
        factor = jnp.exp(level[1] - top)
        numer = numer + level[0] * factor[..., None]
        total = total + level[2] * factor
    attended = (
        jnp.transpose(numer / total[..., None], (1, 0, 2))
        .reshape(tok_rows, -1)
        .astype(jnp.bfloat16)
    )
    terms = jnp.dot(attended, out_weight, preferred_element_type=jnp.float32)
    return lax.psum_scatter(terms.astype(jnp.bfloat16), "head", scatter_dimension=1, tiled=True)


def solution(mesh):
    placed = (P("seq", "head"), P("seq", "head"), P("seq", "head"), P("head", None))

    def whole(queries, keys, values, out_weight):
        body = fast_shards if fits_fast(mesh, queries) else shards
        mapped = jax.shard_map(body, mesh=mesh, in_specs=placed, out_specs=P("seq", "head"), check_vma=False)
        return mapped(queries, keys, values, out_weight)

    return whole
```

```python
import functools
import math

import jax
import jax.numpy as jnp
from jax import lax
from jax.experimental import pallas as pl
from jax.experimental.pallas import tpu as pltpu
from jax.sharding import PartitionSpec as P

HEAD_DIM = 128
SEG1 = 2048
SEG2 = 8192


NEG_FILL = -1e30
LOG2_SCALE = math.log2(math.e) / math.sqrt(HEAD_DIM)
CHUNK = 256
GROUP = 8
MID_ROWS = CHUNK // 4
FAR_ROWS = CHUNK // 16
STAT_ROWS = 16
VMEM_BYTES = 50 * 2**20
COST_CUT = 64
F32 = jnp.float32
BF16 = jnp.bfloat16


def iota(shape, dim):
    return lax.broadcasted_iota(jnp.int32, shape, dim)


def token_of_row(row):
    return 16 * (row & 15) + 4 * ((row >> 4) & 3) + (row >> 6)


def mid_of_row(row):
    return (row >> 6) * 64 + 4 * (row & 15) + ((row >> 4) & 3)


def dot(lhs, rhs):
    return lax.dot_general(lhs, rhs, (((1,), (0,)), ((), ())), preferred_element_type=F32)


def dot_t(lhs, rhs):
    return lax.dot_general(lhs, rhs, (((1,), (1,)), ((), ())), preferred_element_type=F32)


def with_ones(values):
    return jnp.concatenate([values, jnp.ones_like(values)], axis=1)


def attend_all(items):
    def scores(item):
        query = item[0]()
        found = []
        for keys, _, mask in item[1]():
            score = dot_t(query, keys())
            found.append(score if mask is None else jnp.where(mask, score, NEG_FILL))
        return found

    def weigh(found):
        peak = None
        for score in found:
            top = jnp.max(score, axis=1, keepdims=True)
            peak = top if peak is None else jnp.maximum(peak, top)
        return [jnp.exp2((score - peak) * LOG2_SCALE).astype(BF16) for score in found], peak

    def finish(item, weights, peak):
        acc = None
        for weight, (_, values, _) in zip(weights, item[1]()):
            term = dot(weight, with_ones(values()))
            acc = term if acc is None else acc + term
        total = acc[:, HEAD_DIM:]
        item[2](acc[:, :HEAD_DIM] / total, peak * LOG2_SCALE + jnp.log2(total))

    found = scores(items[0])
    waiting = None
    for n, item in enumerate(items):
        following = scores(items[n + 1]) if n + 1 < len(items) else None
        weights, peak = weigh(found)
        if waiting is not None:
            finish(*waiting)
        waiting = (item, weights, peak)
        found = following
    finish(*waiting)


def merge(out_a, lse_a, out_b, lse_b):
    top = jnp.maximum(lse_a, lse_b)
    fac_a = jnp.exp2(lse_a - top)
    fac_b = jnp.exp2(lse_b - top)
    total = fac_a + fac_b
    return (out_a * fac_a + out_b * fac_b) / total, top + jnp.log2(total)


def pick_rows(source, owner):
    row = iota((2 * MID_ROWS, CHUNK), 0)
    residue = 2 * (owner & 1) + (row >> 6)
    token = 16 * (row & 15) + 4 * ((row >> 4) & 3) + residue
    pick = (token == iota((2 * MID_ROWS, CHUNK), 1)).astype(F32).astype(BF16)
    both = dot(pick, source[:, owner * 256 : (owner + 1) * 256])
    return jnp.concatenate([both[:MID_ROWS, :128], both[MID_ROWS:, 128:]], axis=1).astype(BF16)


def prep_kernel(chunks, place, k_ref, v_ref, q_ref, blocks_ref, high_ref, far_ref):
    chunk = pl.program_id(0)
    for owner in range(GROUP):
        blocks_ref[owner, chunk] = pick_rows(k_ref, owner)
        blocks_ref[owner, chunks + chunk] = pick_rows(v_ref, owner)
    half = chunks // 2

    @pl.when(chunk < half)
    def _():
        for owner in range(GROUP):
            blocks_ref[owner, 2 * chunks + chunk] = pick_rows(q_ref, owner)

    @pl.when(chunk >= half)
    def _():
        for owner in range(GROUP):
            high_ref[owner, chunk - half] = pick_rows(q_ref, owner)

    at = pl.multiple_of(chunk * FAR_ROWS, FAR_ROWS)
    for owner in range(GROUP):
        start = ((owner >> 1) & 3) * FAR_ROWS
        for a in range(2):
            far_ref[owner, a, pl.ds(at, FAR_ROWS), :] = blocks_ref[
                owner, a * chunks + chunk, start : start + FAR_ROWS, :
            ]


def reorder_kernel(place, q_ref, rows_ref):
    row = iota((CHUNK, CHUNK), 0)
    pick = (token_of_row(row) == iota((CHUNK, CHUNK), 1)).astype(F32).astype(BF16)
    rows_ref[...] = dot(pick, q_ref[...]).astype(BF16)


def gate_kernel(place):
    pass


def near_kernel(part, per_step, first_head, place, q_ref, k_ref, v_ref, pk_ref, pv_ref, o_ref, lse_ref):
    step = pl.program_id(0)
    second = (place[0] & 1) == 1

    @pl.when(step == 0)
    def _():
        lse_ref[...] = jnp.zeros_like(lse_ref)

    mask = token_of_row(iota((CHUNK, CHUNK), 0)) >= iota((CHUNK, CHUNK), 1)

    def run(with_prev):
        items = []
        for e in range(per_step):
            lanes = slice(e * 128, (e + 1) * 128)
            for c in range(2):
                before = (2 * part + c) * CHUNK
                here = slice(c * CHUNK, (c + 1) * CHUNK)

                def query(here=here, lanes=lanes):
                    return q_ref[here, lanes]

                def pair(ref_k, ref_v, rows, mask, lanes=lanes):
                    return (lambda: ref_k[rows, lanes], lambda: ref_v[rows, lanes], mask)

                def parts(before=before, pair=pair):
                    found = [pair(k_ref, v_ref, slice(before, before + CHUNK), mask)]
                    if before:
                        found.append(pair(k_ref, v_ref, slice(0, before), None))
                    if with_prev:
                        found.append(pair(pk_ref, pv_ref, slice(None), None))
                    return found

                def store(out, lse, e=e, c=c, here=here, lanes=lanes):
                    o_ref[here, lanes] = out.astype(BF16)
                    residue = e % 4
                    kept = lse[residue * MID_ROWS : (residue + 1) * MID_ROWS]
                    head = first_head + step * per_step + e
                    lse_ref[c] = jnp.where(iota((MID_ROWS, 128), 1) == head, kept, lse_ref[c])

                items.append((query, parts, store))
        attend_all(items)

    @pl.when(second)
    def _():
        run(True)

    @pl.when(jnp.logical_not(second))
    def _():
        run(False)


def mid_kernel(part, chunks, place, kvq, *refs):
    me = place[0]
    segment = place[1]
    rows = chunks * MID_ROWS
    half = rows // 2
    if part:
        q, refs = refs[0], refs[1:]
        q_first = 0
    else:
        q, q_first = kvq, 2 * chunks
    far, out_ref, res, lses = refs

    def query_rows(i, lanes):
        return q[i, q_first : q_first + chunks // 2, :, lanes].reshape(half, 128)

    def kv_rows(a, devices, count, lanes):
        found = kvq[devices, a * chunks : a * chunks + count, :, lanes]
        return found.reshape(-1, 128)

    own = (part + 1) * half
    mask = mid_of_row(iota((half, own), 0) + part * half) >= mid_of_row(iota((half, own), 1))
    items = []
    for e in range(2):
        lanes = slice(e * 128, (e + 1) * 128)
        for i in range(GROUP):

            def query(i=i, lanes=lanes):
                return query_rows(i, lanes)

            def parts(i=i, lanes=lanes):
                seen = (part + 1) * chunks // 2
                here, before = slice(i, i + 1), slice(0, i)
                found = [(lambda: kv_rows(0, here, seen, lanes), lambda: kv_rows(1, here, seen, lanes), mask)]
                if i:
                    found.append(
                        (lambda: kv_rows(0, before, chunks, lanes), lambda: kv_rows(1, before, chunks, lanes), None)
                    )
                return found

            def store(out, lse, e=e, i=i):
                res[e, i] = out
                lses[e, i] = lse

            items.append((query, parts, store))
    attend_all(items)

    start = pl.multiple_of(((me >> 1) & 3) * FAR_ROWS, FAR_ROWS)
    count = GROUP * chunks * FAR_ROWS
    asked = count // 2
    row = iota((asked, count), 0)
    per_part = chunks // 2 * FAR_ROWS
    position = row // per_part * chunks * FAR_ROWS + part * per_part + row % per_part
    mask = position >= iota((asked, count), 1)
    other_mask = jnp.broadcast_to(segment == 1, (asked, count))
    items = []
    for e in range(2):
        lanes = slice(e * 128, (e + 1) * 128)

        def gathered(ref, first, count, lanes=lanes):
            found = ref[:, first : first + count, pl.ds(start, FAR_ROWS), lanes]
            return found.reshape(GROUP * count * FAR_ROWS, 128)

        def query(gathered=gathered):
            return gathered(q, q_first, chunks // 2)

        def other(a, lanes=lanes):
            return far[:, a, :, lanes].reshape(count, 128)

        def parts(gathered=gathered, other=other):
            return [
                (lambda: gathered(kvq, 0, chunks), lambda: gathered(kvq, chunks, chunks), mask),
                (lambda: other(0), lambda: other(1), other_mask),
            ]

        def store(out, lse, e=e):
            for i in range(GROUP):
                for c in range(chunks // 2):
                    at = pl.ds(start + c * MID_ROWS, FAR_ROWS)
                    piece = slice((i * 2 + c) * FAR_ROWS, (i * 2 + c + 1) * FAR_ROWS)
                    res[e, i, at, :], lses[e, i, at, :] = merge(
                        res[e, i, at, :], lses[e, i, at, :], out[piece], lse[piece]
                    )

        items.append((query, parts, store))
    attend_all(items)

    lane = iota((half, 128), 1)
    stats = jnp.zeros((half, 128), F32)
    for d in range(GROUP):
        for e in range(2):
            stats = jnp.where(lane == 8 * d + e, lses[e, d], stats)
            out_ref[d, :half, e * 128 : (e + 1) * 128] = res[e, d].astype(BF16)
    stats = jnp.transpose(stats)
    high = stats.astype(BF16).astype(F32)
    low = stats - high
    for d in range(GROUP):
        tile = jnp.concatenate([high[8 * d : 8 * d + 8], low[8 * d : 8 * d + 8]], axis=0)
        out_ref[d, half:, :] = jnp.concatenate([tile, jnp.zeros_like(tile)], axis=1).astype(BF16)


def combine_kernel(half, chunk, pieces, place, *refs):
    near = refs[:pieces]
    lses = refs[pieces : 2 * pieces]
    back, w_ref, send_ref, att_ref, work = refs[2 * pieces :]

    @pl.when(pl.program_id(0) == 0)
    def _():
        wide = near[0].shape[1]
        stats = []
        for d in range(GROUP):
            tile = back[d, half:, :128].astype(F32)
            stats.append(tile[:8] + tile[8:])
        stats.append(jnp.zeros((128 - 8 * GROUP, 128), F32))
        stats = jnp.transpose(jnp.concatenate(stats, axis=0))
        first = chunk % 2 * MID_ROWS
        stats = stats[first : first + MID_ROWS]
        for n in range(pieces):
            work[:, n * wide : (n + 1) * wide] = near[n][...]
        for d in range(GROUP):
            for e in range(2):
                start = (2 * (d & 1) + e) * MID_ROWS
                column = d * 256 + e * 128
                at = (slice(start, start + MID_ROWS), slice(column, column + 128))
                near_lse = lses[column // wide][0, :, 2 * d + e : 2 * d + e + 1]
                mid = back[d, first : first + MID_ROWS, e * 128 : (e + 1) * 128]
                mid_lse = stats[:, 8 * d + e : 8 * d + e + 1]
                out, _ = merge(work[at].astype(F32), near_lse, mid.astype(F32), mid_lse)
                work[at] = out.astype(BF16)
        row = token_of_row(iota((CHUNK, CHUNK), 1))
        pick = (row == iota((CHUNK, CHUNK), 0)).astype(F32).astype(BF16)
        att_ref[...] = dot(pick, work[...]).astype(BF16)

    send_ref[...] = dot(att_ref[...], w_ref[...]).astype(BF16)


def project_kernel(chunks, place, *refs):
    attended = refs[:chunks]
    w_ref, out_ref = refs[chunks:]
    for c in range(chunks):
        out_ref[c * CHUNK : (c + 1) * CHUNK, :] = dot(attended[c][...], w_ref[...]).astype(BF16)


def call(
    kernel, place, args, in_specs, out_specs, out_shape, grid, scratch=(), after=(), carry=(), flops=0, moved=0, name=None
):
    count = len(args)
    outputs = len(out_shape)
    extra = len(after) + len(carry)
    anywhere = pl.BlockSpec(memory_space=pl.ANY)

    def body(place_ref, *refs):
        results = refs[count + extra :]
        kernel(place_ref, *refs[:count], *results[:outputs], *results[outputs + len(carry) :])

    return pl.pallas_call(
        body,
        grid_spec=pltpu.PrefetchScalarGridSpec(
            num_scalar_prefetch=1,
            grid=grid,
            in_specs=list(in_specs) + [anywhere] * extra,
            out_specs=list(out_specs) + [anywhere] * len(carry),
            scratch_shapes=scratch,
        ),
        out_shape=list(out_shape) + [jax.ShapeDtypeStruct(a.shape, a.dtype) for a in carry],
        input_output_aliases={1 + count + len(after) + n: outputs + n for n in range(len(carry))},
        compiler_params=pltpu.CompilerParams(vmem_limit_bytes=VMEM_BYTES),
        cost_estimate=pl.CostEstimate(flops=flops // COST_CUT, bytes_accessed=moved // COST_CUT, transcendentals=0),
        name=name,
    )(place, *args, *after, *carry)


def fast_shards(queries, keys, values, out_weight):
    tokens, width = queries.shape
    heads = width // HEAD_DIM
    features = out_weight.shape[1]
    chunks = tokens // CHUNK
    mid_rows = tokens // 4
    far_rows = tokens // 16
    half = mid_rows // 2
    seq_size = lax.axis_size("seq")
    seq_index = lax.axis_index("seq")
    place = jnp.stack([seq_index % GROUP, seq_index // GROUP, lax.axis_index("head")]).astype(jnp.int32)
    segments = [list(range(n, n + GROUP)) for n in range(0, seq_size, GROUP)]
    spec = pl.BlockSpec

    def array(*dims, kind=BF16):
        return jax.ShapeDtypeStruct(dims, kind)

    def whole(*dims):
        return spec(dims, lambda n, p: (0,) * len(dims))

    def exchange(blocks):
        return lax.all_to_all(blocks, "seq", 0, 0, axis_index_groups=segments, tiled=True)

    by_chunk = spec((CHUNK, width), lambda c, p: (c, 0))
    blocks_shape = (GROUP, 2 * chunks + chunks // 2, MID_ROWS, 256)
    high_shape = (GROUP, chunks // 2, MID_ROWS, 256)
    far_shape = (GROUP, 2, far_rows, 256)
    blocks, q_high, far = call(
        functools.partial(prep_kernel, chunks),
        place,
        (keys, values, queries),
        [by_chunk] * 3,
        [whole(*blocks_shape), whole(*high_shape), whole(*far_shape)],
        [array(*blocks_shape), array(*high_shape), array(*far_shape)],
        (chunks,),
        flops=3 * 2 * tokens * 2 * MID_ROWS * width,
        moved=16 * 2**20,
        name="prep",
    )
    blocks = exchange(blocks)
    far = lax.ppermute(far, "seq", [(i, (i + GROUP) % seq_size) for i in range(seq_size)])
    pairs = [(i, i + 1) for i in range(0, seq_size, 2)]
    prev_k = lax.ppermute(keys, "seq", pairs)
    prev_v = lax.ppermute(values, "seq", pairs)
    (ordered,) = call(
        reorder_kernel,
        place,
        (queries,),
        [by_chunk],
        [by_chunk],
        [array(tokens, width)],
        (chunks,),
        after=[q_high],
        flops=2 * tokens * CHUNK * width,
        moved=8 * 2**20,
        name="reorder",
    )

    def near(part, first_head, head_count, after=()):
        per_step = 4
        steps = head_count // per_step
        rows = tokens // 2
        wide = per_step * HEAD_DIM
        offset = first_head // per_step

        def columns(count, block):
            return spec((count, wide), lambda s, p: (block, offset + s))

        return call(
            functools.partial(near_kernel, part, per_step, first_head),
            place,
            (ordered, keys, values, prev_k, prev_v),
            [columns(rows, part)] + [columns(rows * (part + 1), 0)] * 2 + [columns(tokens, 0)] * 2,
            [spec((rows, wide), lambda s, p: (0, s)), whole(2, MID_ROWS, 128)],
            [array(rows, head_count * HEAD_DIM), array(2, MID_ROWS, 128, kind=F32)],
            (steps,),
            after=after,
            flops=4 * head_count * rows * (tokens + rows * (part + 1)) * HEAD_DIM,
            moved=2 * head_count * HEAD_DIM * (2 * rows + 4 * tokens),
            name="near",
        )

    back_shape = (GROUP, half + STAT_ROWS, 256)

    def mid(part, after=()):
        return call(
            functools.partial(mid_kernel, part, chunks),
            place,
            (blocks, *([q_high] if part else []), far),
            [whole(*blocks_shape)] + [whole(*high_shape)] * part + [whole(*far_shape)],
            [whole(*back_shape)],
            [array(*back_shape)],
            (1,),
            scratch=[pltpu.VMEM((2, GROUP, half, 128), F32), pltpu.VMEM((2, GROUP, half, 128), F32)],
            after=after,
            flops=2 * 2 * (GROUP * mid_rows) ** 2 // 2 * HEAD_DIM,
            moved=4 * 2**20,
            name="mid",
        )[0]

    out_half = features // 2
    tile = 1024
    tiles = out_half // tile

    def combine(chunk, near_parts, back, after=(), carry=()):
        count = len(near_parts)
        wide = width // count
        local = chunk % 2
        return call(
            functools.partial(combine_kernel, half, chunk, count),
            place,
            (*[o for o, _ in near_parts], *[lse for _, lse in near_parts], back, out_weight),
            [spec((CHUNK, wide), lambda n, p: (local, 0))] * count
            + [spec((1, MID_ROWS, 128), lambda n, p: (local, 0, 0))] * count
            + [whole(*back_shape), spec((width, tile), lambda n, p: (0, (1 - p[2]) * tiles + n))],
            [spec((CHUNK, tile), lambda n, p: (0, n)), whole(CHUNK, width)],
            [array(CHUNK, out_half), array(CHUNK, width)],
            (tiles,),
            scratch=[pltpu.VMEM((CHUNK, width), BF16)],
            after=after,
            carry=carry,
            flops=2 * CHUNK * width * out_half,
            moved=2 * width * out_half,
            name="combine",
        )

    def project(attended, after=()):
        own_tile = 512
        own_tiles = out_half // own_tile
        rows = CHUNK * len(attended)
        return call(
            functools.partial(project_kernel, len(attended)),
            place,
            (*attended, out_weight),
            [whole(CHUNK, width)] * len(attended)
            + [spec((width, own_tile), lambda n, p: (0, p[2] * own_tiles + n))],
            [spec((rows, own_tile), lambda n, p: (0, n))],
            [array(rows, out_half)],
            (own_tiles,),
            after=after,
            flops=2 * rows * width * out_half,
            moved=2 * (width + 2 * rows) * out_half,
            name="project",
        )[0]

    def swapped(sent):
        return lax.ppermute(sent, "head", [(0, 1), (1, 0)])

    near_low = [near(0, 0, heads // 2)]
    (far,) = call(gate_kernel, place, (), [], [], [], (1,), after=[blocks, near_low[0][1]], carry=[far], name="gate")
    far = exchange(far)
    near_low.append(near(0, heads // 2, heads // 2, after=[near_low[0][1]]))
    mid_low = mid(0, after=[near_low[1][1]])
    back_low = exchange(mid_low)
    near_high = [near(1, 0, heads // 2, after=[mid_low])]
    send0, att0 = combine(0, near_low, back_low, after=[near_high[0][1]])
    recv0 = swapped(send0)
    send1, att1, q_high = combine(1, near_low, back_low, after=[send0], carry=[q_high])
    recv1 = swapped(send1)
    q_high = exchange(q_high)
    near_high.append(near(1, heads // 2, heads // 2, after=[send1]))
    mid_high = mid(1, after=[near_high[1][1]])
    back_high = exchange(mid_high)
    own_low = project([att0, att1], after=[mid_high])
    send2, att2 = combine(2, near_high, back_high, after=[own_low, recv0, recv1])
    recv2 = swapped(send2)
    send3, att3 = combine(3, near_high, back_high, after=[send2])
    recv3 = swapped(send3)
    own_high = project([att2, att3], after=[send3])
    mixed = jnp.concatenate([own_low, own_high], axis=0)
    for c, received in enumerate((recv0, recv1, recv2, recv3)):
        own = lax.slice_in_dim(mixed, c * CHUNK, (c + 1) * CHUNK, axis=0)
        total = (own.astype(F32) + received.astype(F32)).astype(BF16)
        mixed = lax.dynamic_update_slice_in_dim(mixed, total, c * CHUNK, axis=0)
    return mixed


def fits_fast(mesh, queries):
    seq, head = mesh.shape["seq"], mesh.shape["head"]
    tokens = queries.shape[0] // seq
    heads = queries.shape[1] // HEAD_DIM // head
    return (
        head == 2
        and heads == 2 * GROUP
        and seq == 2 * GROUP
        and tokens == 4 * CHUNK
        and SEG1 == 2 * tokens
        and SEG2 == GROUP * tokens
    )


def passed_along(value, axis, steps):
    count = lax.axis_size(axis)
    leading, last = (max(0, -steps), min(count, count - steps))
    return lax.ppermute(value, axis, [(source, source + steps) for source in range(leading, last)])


def attend_block(query, key_rows, value_rows, valid, scale):
    scores = jnp.einsum("qhd,khd->hqk", query, key_rows, preferred_element_type=jnp.float32) * scale
    scores = jnp.where(valid, scores, NEG_FILL)
    peak = jnp.max(scores, axis=-1)
    weights = jnp.where(valid, jnp.exp(scores - peak[..., None]), 0.0)
    total = jnp.sum(weights, axis=-1)
    numer = jnp.einsum(
        "hqk,khd->hqd", weights.astype(jnp.bfloat16), value_rows, preferred_element_type=jnp.float32
    )
    return (numer, peak, total)


def absorb_block(state, query, key_rows, value_rows, valid, scale):
    numer, peak, total = state
    scores = jnp.einsum("qhd,khd->hqk", query, key_rows, preferred_element_type=jnp.float32) * scale
    scores = jnp.where(valid, scores, NEG_FILL)
    new_peak = jnp.maximum(peak, jnp.max(scores, axis=-1))
    weights = jnp.where(valid, jnp.exp(scores - new_peak[..., None]), 0.0)
    added = jnp.einsum(
        "hqk,khd->hqd", weights.astype(jnp.bfloat16), value_rows, preferred_element_type=jnp.float32
    )
    return (added, new_peak, jnp.sum(weights, axis=-1))


def take_dilated(source, stride, offsets):
    count = source.shape[0] // stride
    shaped = source.reshape(count, stride, offsets.shape[0], -1)
    picker = (jnp.arange(stride)[:, None] == offsets[None, :]).astype(source.dtype)
    return jnp.sum(shaped * picker[None, :, :, None], axis=1).reshape(count, -1)


def spread_rows(state, stride, offsets):
    numer, peak, total = state
    heads_here, count = peak.shape
    picker = jnp.arange(stride)[None, :] == offsets[:, None]
    numer_full = jnp.where(picker[:, None, :, None], numer[:, :, None, :], 0.0).reshape(
        heads_here, count * stride, -1
    )
    peak_full = jnp.where(picker[:, None, :], peak[:, :, None], NEG_FILL).reshape(
        heads_here, count * stride
    )
    total_full = jnp.where(picker[:, None, :], total[:, :, None], 0.0).reshape(
        heads_here, count * stride
    )
    return (numer_full, peak_full, total_full)


def shards(queries, keys, values, out_weight):
    tok_rows = queries.shape[0]
    heads_here = queries.shape[1] // HEAD_DIM
    scale = 1.0 / math.sqrt(HEAD_DIM)
    seq_index = lax.axis_index("seq")
    head_index = lax.axis_index("head")
    head_ids = head_index * heads_here + jnp.arange(heads_here)
    query_pos = seq_index * tok_rows + jnp.arange(tok_rows)
    near_span = SEG1 // tok_rows
    near_keys, near_values = (keys, values)
    level_bit = 0
    moved = passed_along((near_keys, near_values), "seq", 1 << level_bit)
    near_keys = jnp.concatenate([moved[0], near_keys], axis=0)
    near_values = jnp.concatenate([moved[1], near_values], axis=0)
    near_pos = (seq_index - near_span + 1) * tok_rows + jnp.arange(near_span * tok_rows)
    near_start = seq_index // near_span * near_span * tok_rows
    near_valid = (near_pos[None, :] <= query_pos[:, None]) & (near_pos[None, :] >= near_start)

    def near_head(head_slot):
        column = head_slot * HEAD_DIM
        query = lax.dynamic_slice_in_dim(queries, column, HEAD_DIM, 1)[:, None, :]
        key_rows = lax.dynamic_slice_in_dim(near_keys, column, HEAD_DIM, 1)[:, None, :]
        value_rows = lax.dynamic_slice_in_dim(near_values, column, HEAD_DIM, 1)[:, None, :]
        numer, peak, total = attend_block(query, key_rows, value_rows, near_valid[None], scale)
        return (numer[0], peak[0], total[0])

    near_state = lax.map(near_head, jnp.arange(heads_here))
    mid_offsets = head_ids % 4
    far_offsets = head_ids % 16
    mid_count = tok_rows // 4
    far_count = tok_rows // 16
    mid_query = take_dilated(queries, 4, mid_offsets).reshape(mid_count, heads_here, HEAD_DIM)
    far_query = take_dilated(queries, 16, far_offsets).reshape(far_count, heads_here, HEAD_DIM)
    mid_keys = take_dilated(keys, 4, mid_offsets)
    mid_values = take_dilated(values, 4, mid_offsets)
    mid_qpos = seq_index * tok_rows + mid_offsets[:, None] + 4 * jnp.arange(mid_count)[None, :]
    far_qpos = seq_index * tok_rows + far_offsets[:, None] + 16 * jnp.arange(far_count)[None, :]
    mid_span = SEG2 // tok_rows
    mid_start = seq_index // mid_span * mid_span * tok_rows
    empty_far = (
        jnp.zeros((heads_here, far_count, HEAD_DIM), jnp.float32),
        jnp.full((heads_here, far_count), NEG_FILL, jnp.float32),
        jnp.zeros((heads_here, far_count), jnp.float32),
    )
    block_keys, block_values = (mid_keys, mid_values)
    for level_bit in range(mid_span.bit_length() - 1):
        moved = passed_along((block_keys, block_values), "seq", 1 << level_bit)
        block_keys = jnp.concatenate([moved[0], block_keys], axis=0)
        block_values = jnp.concatenate([moved[1], block_values], axis=0)
    key_index = jnp.arange(mid_span * mid_count)
    mid_kpos = (
        (seq_index - mid_span + 1) * tok_rows
        + (key_index // mid_count * tok_rows + 4 * (key_index % mid_count))[None, :]
        + mid_offsets[:, None]
    )
    mid_valid = (mid_kpos[:, None, :] <= mid_qpos[:, :, None]) & (mid_kpos[:, None, :] >= mid_start)
    mid_state = attend_block(
        mid_query,
        block_keys.reshape(-1, heads_here, HEAD_DIM),
        block_values.reshape(-1, heads_here, HEAD_DIM),
        mid_valid,
        scale,
    )
    far_keys = take_dilated(keys, 16, far_offsets)
    far_values = take_dilated(values, 16, far_offsets)
    piece = (
        lax.all_gather(far_keys, "seq", axis=0, tiled=True),
        lax.all_gather(far_values, "seq", axis=0, tiled=True),
    )
    count = piece[0].shape[0]
    row_index = jnp.arange(count)
    key_pos = (row_index // far_count * tok_rows + 16 * (row_index % far_count))[
        None, :
    ] + far_offsets[:, None]
    valid = key_pos[:, None, :] <= far_qpos[:, :, None]
    far_state = absorb_block(
        empty_far,
        far_query,
        piece[0].reshape(count, heads_here, HEAD_DIM),
        piece[1].reshape(count, heads_here, HEAD_DIM),
        valid,
        scale,
    )
    levels = (
        near_state,
        spread_rows(mid_state, 4, mid_offsets),
        spread_rows(far_state, 16, far_offsets),
    )
    top = jnp.maximum(jnp.maximum(levels[0][1], levels[1][1]), levels[2][1])
    numer = jnp.zeros_like(levels[0][0])
    total = jnp.zeros_like(levels[0][2])
    for level in levels:
        factor = jnp.exp(level[1] - top)
        numer = numer + level[0] * factor[..., None]
        total = total + level[2] * factor
    attended = (
        jnp.transpose(numer / total[..., None], (1, 0, 2))
        .reshape(tok_rows, -1)
        .astype(jnp.bfloat16)
    )
    terms = jnp.dot(attended, out_weight, preferred_element_type=jnp.float32)
    return lax.psum_scatter(terms.astype(jnp.bfloat16), "head", scatter_dimension=1, tiled=True)


def solution(mesh):
    placed = (P("seq", "head"), P("seq", "head"), P("seq", "head"), P("head", None))

    def whole(queries, keys, values, out_weight):
        body = fast_shards if fits_fast(mesh, queries) else shards
        mapped = jax.shard_map(body, mesh=mesh, in_specs=placed, out_specs=P("seq", "head"), check_vma=False)
        return mapped(queries, keys, values, out_weight)

    return whole
```

```python
import functools
import math

import jax
import jax.numpy as jnp
from jax import lax
from jax.experimental import pallas as pl
from jax.experimental.pallas import tpu as pltpu
from jax.sharding import PartitionSpec as P

HEAD_DIM = 128
SEG1 = 2048
SEG2 = 8192


NEG_FILL = -1e30
LOG2_SCALE = math.log2(math.e) / math.sqrt(HEAD_DIM)
CHUNK = 256
GROUP = 8
MID_ROWS = CHUNK // 4
FAR_ROWS = CHUNK // 16
STAT_ROWS = 16
VMEM_BYTES = 127 * 2**19
COST_CUT = 64
F32 = jnp.float32
BF16 = jnp.bfloat16


def iota(shape, dim):
    return lax.broadcasted_iota(jnp.int32, shape, dim)


def token_of_row(row):
    return 16 * (row & 15) + 4 * ((row >> 4) & 3) + (row >> 6)


def mid_of_row(row):
    return (row >> 6) * 64 + 4 * (row & 15) + ((row >> 4) & 3)


def dot(lhs, rhs):
    return lax.dot_general(lhs, rhs, (((1,), (0,)), ((), ())), preferred_element_type=F32)


def dot_t(lhs, rhs):
    return lax.dot_general(lhs, rhs, (((1,), (1,)), ((), ())), preferred_element_type=F32)


def with_ones(values):
    return jnp.concatenate([values, jnp.ones_like(values)], axis=1)


def attend_all(items):
    def scores(item):
        query = item[0]()
        found = []
        for keys, _, mask in item[1]():
            score = dot_t(query, keys())
            found.append(score if mask is None else jnp.where(mask, score, NEG_FILL))
        return found

    def weigh(found):
        peak = None
        for score in found:
            top = jnp.max(score, axis=1, keepdims=True)
            peak = top if peak is None else jnp.maximum(peak, top)
        return [jnp.exp2((score - peak) * LOG2_SCALE).astype(BF16) for score in found], peak

    def finish(item, weights, peak):
        acc = None
        for weight, (_, values, _) in zip(weights, item[1]()):
            term = dot(weight, with_ones(values()))
            acc = term if acc is None else acc + term
        total = acc[:, HEAD_DIM:]
        item[2](acc[:, :HEAD_DIM] / total, peak * LOG2_SCALE + jnp.log2(total))

    found = scores(items[0])
    waiting = None
    for n, item in enumerate(items):
        following = scores(items[n + 1]) if n + 1 < len(items) else None
        weights, peak = weigh(found)
        if waiting is not None:
            finish(*waiting)
        waiting = (item, weights, peak)
        found = following
    finish(*waiting)


def merge(out_a, lse_a, out_b, lse_b):
    top = jnp.maximum(lse_a, lse_b)
    fac_a = jnp.exp2(lse_a - top)
    fac_b = jnp.exp2(lse_b - top)
    total = fac_a + fac_b
    return (out_a * fac_a + out_b * fac_b) / total, top + jnp.log2(total)


def pick_rows(source, owner):
    row = iota((2 * MID_ROWS, CHUNK), 0)
    residue = 2 * (owner & 1) + (row >> 6)
    token = 16 * (row & 15) + 4 * ((row >> 4) & 3) + residue
    pick = (token == iota((2 * MID_ROWS, CHUNK), 1)).astype(F32).astype(BF16)
    both = dot(pick, source[:, owner * 256 : (owner + 1) * 256])
    return jnp.concatenate([both[:MID_ROWS, :128], both[MID_ROWS:, 128:]], axis=1).astype(BF16)


def prep_kernel(chunks, place, k_ref, v_ref, q_ref, blocks_ref, far_ref):
    chunk = pl.program_id(0)
    at = pl.multiple_of(chunk * FAR_ROWS, FAR_ROWS)
    for owner in range(GROUP):
        start = ((owner >> 1) & 3) * FAR_ROWS
        for a, source in enumerate((k_ref, v_ref, q_ref)):
            rows = pick_rows(source, owner)
            blocks_ref[owner, a * chunks + chunk] = rows
            if a < 2:
                far_ref[owner, a, pl.ds(at, FAR_ROWS), :] = rows[start : start + FAR_ROWS]


def reorder_kernel(place, q_ref, rows_ref):
    row = iota((CHUNK, CHUNK), 0)
    pick = (token_of_row(row) == iota((CHUNK, CHUNK), 1)).astype(F32).astype(BF16)
    rows_ref[...] = dot(pick, q_ref[...]).astype(BF16)


def gate_kernel(place):
    pass


def fill_kernel(place, far_ref, blocks_ref):
    blocks_ref[...] = far_ref[...]


def near_kernel(part, per_step, first_head, place, q_ref, k_ref, v_ref, pk_ref, pv_ref, done_ref, kept_ref, lse_ref):
    step = pl.program_id(0)
    second = (place[0] & 1) == 1

    @pl.when(step == 0)
    def _():
        lse_ref[...] = jnp.zeros_like(lse_ref)

    token, column = token_of_row(iota((CHUNK, CHUNK), 0)), iota((CHUNK, CHUNK), 1)
    mask = token >= column

    def run(with_prev):
        items = []
        for e in range(per_step):
            lanes = slice(e * 128, (e + 1) * 128)
            for c in range(2):
                before = (2 * part + c) * CHUNK
                here = slice(c * CHUNK, (c + 1) * CHUNK)

                def query(here=here, lanes=lanes):
                    return q_ref[here, lanes]

                def pair(ref_k, ref_v, rows, mask, lanes=lanes):
                    return (lambda: ref_k[rows, lanes], lambda: ref_v[rows, lanes], mask)

                def parts(before=before, pair=pair):
                    found = [pair(k_ref, v_ref, slice(before, before + CHUNK), mask)]
                    if before:
                        found.append(pair(k_ref, v_ref, slice(0, before), None))
                    if with_prev:
                        found.append(pair(pk_ref, pv_ref, slice(None), None))
                    return found

                def store(out, lse, e=e, c=c, here=here, lanes=lanes):
                    residue = e % 4
                    out = out.astype(BF16)
                    for n, other in enumerate(r for r in range(4) if r != residue):
                        done_ref[c, n * MID_ROWS : (n + 1) * MID_ROWS, lanes] = out[
                            other * MID_ROWS : (other + 1) * MID_ROWS
                        ]
                    kept_ref[c, :, lanes] = out[residue * MID_ROWS : (residue + 1) * MID_ROWS]
                    kept = lse[residue * MID_ROWS : (residue + 1) * MID_ROWS]
                    head = first_head + step * per_step + e
                    lse_ref[c] = jnp.where(iota((MID_ROWS, 128), 1) == head, kept, lse_ref[c])

                items.append((query, parts, store))
        attend_all(items)

    @pl.when(second)
    def _():
        run(True)

    @pl.when(jnp.logical_not(second))
    def _():
        run(False)


def halves_kernel(place, first_ref, second_ref, first_out, second_out):
    first_out[...] = first_ref[...]
    second_out[...] = second_ref[...]


def mid_kernel(chunks, place, blocks, out_ref, res, lses):
    me = place[0]
    segment = place[1]
    rows = chunks * MID_ROWS

    def taken(a, devices, lanes):
        return blocks[devices, a * chunks : (a + 1) * chunks, :, lanes].reshape(-1, 128)

    mask = mid_of_row(iota((rows, rows), 0)) >= mid_of_row(iota((rows, rows), 1))
    items = []
    for e in range(2):
        lanes = slice(e * 128, (e + 1) * 128)
        for i in range(GROUP):
            here, before = slice(i, i + 1), slice(0, i)

            def query(here=here, lanes=lanes):
                return taken(2, here, lanes)

            def parts(here=here, before=before, lanes=lanes):
                found = [(lambda: taken(0, here, lanes), lambda: taken(1, here, lanes), mask)]
                if before.stop:
                    found.append((lambda: taken(0, before, lanes), lambda: taken(1, before, lanes), None))
                return found

            def store(out, lse, e=e, i=i):
                res[e, i] = out
                lses[e, i] = lse

            items.append((query, parts, store))
    attend_all(items)

    start = pl.multiple_of(((me >> 1) & 3) * FAR_ROWS, FAR_ROWS)
    count = GROUP * chunks * FAR_ROWS
    mask = iota((count, count), 0) >= iota((count, count), 1)
    other_mask = jnp.broadcast_to(segment == 1, (count, count))
    items = []
    for e in range(2):
        lanes = slice(e * 128, (e + 1) * 128)

        def dilated(a, lanes=lanes):
            found = blocks[:, a * chunks : (a + 1) * chunks, pl.ds(start, FAR_ROWS), lanes]
            return found.reshape(count, 128)

        def other(a, lanes=lanes):
            return blocks[:, 3 * chunks + a, :, lanes].reshape(count, 128)

        def query(dilated=dilated):
            return dilated(2)

        def parts(dilated=dilated, other=other):
            return [
                (lambda: dilated(0), lambda: dilated(1), mask),
                (lambda: other(0), lambda: other(1), other_mask),
            ]

        def store(out, lse, e=e):
            for i in range(GROUP):
                for c in range(chunks):
                    at = pl.ds(start + c * MID_ROWS, FAR_ROWS)
                    first = (i * chunks + c) * FAR_ROWS
                    piece = slice(first, first + FAR_ROWS)
                    res[e, i, at, :], lses[e, i, at, :] = merge(
                        res[e, i, at, :], lses[e, i, at, :], out[piece], lse[piece]
                    )

        items.append((query, parts, store))
    attend_all(items)

    lane = iota((rows, 128), 1)
    stats = jnp.zeros((rows, 128), F32)
    for d in range(GROUP):
        for e in range(2):
            stats = jnp.where(lane == 8 * d + e, lses[e, d], stats)
            out_ref[d, :rows, e * 128 : (e + 1) * 128] = res[e, d].astype(BF16)
    stats = jnp.transpose(stats)
    high = stats.astype(BF16).astype(F32)
    low = stats - high
    for d in range(GROUP):
        out_ref[d, rows:, :] = jnp.concatenate([high[8 * d : 8 * d + 8], low[8 * d : 8 * d + 8]], axis=0).astype(BF16)


def combine_kernel(chunks, place, *refs):
    kept, lses = refs[:4], refs[4:8]
    back, low_ref, high_ref = refs[8:]
    rows = chunks * MID_ROWS
    stats = []
    for d in range(GROUP):
        tile = back[d, rows:, :].astype(F32)
        stats.append((tile[:8] + tile[8:])[:2])
    stats.append(jnp.zeros((128 - 2 * GROUP, rows), F32))
    stats = jnp.transpose(jnp.concatenate(stats, axis=0))
    wide = kept[0].shape[2]
    for c in range(chunks):
        first = c * MID_ROWS
        out_ref = low_ref if c < 2 else high_ref
        near_lse = lses[c // 2 * 2][c % 2] + lses[c // 2 * 2 + 1][c % 2]
        mid_lse = stats[first : first + MID_ROWS]
        top = jnp.maximum(near_lse, mid_lse)
        near_fac = jnp.exp2(near_lse - top)
        mid_fac = jnp.exp2(mid_lse - top)
        total = near_fac + mid_fac
        near_fac = near_fac / total
        mid_fac = mid_fac / total
        for d in range(GROUP):
            for e in range(2):
                column = d * 256 + e * 128
                head = 2 * d + e
                part = c // 2 * 2 + column // wide
                inner = column % wide
                near = kept[part][c % 2, :, inner : inner + 128].astype(F32)
                mid = back[d, first : first + MID_ROWS, e * 128 : (e + 1) * 128].astype(F32)
                out = near * near_fac[:, head : head + 1] + mid * mid_fac[:, head : head + 1]
                out_ref[c % 2, :, column : column + 128] = out.astype(BF16)


def assemble(work, done, joined):
    wide = done[0].shape[2]
    for head in range(2 * GROUP):
        residue = head % 4
        column = head * HEAD_DIM
        lanes = slice(column, column + HEAD_DIM)
        source = done[column // wide]
        inner = column % wide
        for c in range(2):
            for n, other in enumerate(r for r in range(4) if r != residue):
                at = slice(c * CHUNK + other * MID_ROWS, c * CHUNK + (other + 1) * MID_ROWS)
                work[at, lanes] = source[c, n * MID_ROWS : (n + 1) * MID_ROWS, inner : inner + HEAD_DIM]
            at = slice(c * CHUNK + residue * MID_ROWS, c * CHUNK + (residue + 1) * MID_ROWS)
            work[at, lanes] = jnp.zeros((MID_ROWS, HEAD_DIM), BF16) if joined is None else joined[c, :, lanes]


def own_near_kernel(place, *refs):
    done = refs[0:2], refs[2:4]
    w_ref, out_ref, work = refs[4:]

    @pl.when(pl.program_id(0) == 0)
    def _():
        for half in range(2):
            assemble(work.at[half * 2 * CHUNK : (half + 1) * 2 * CHUNK], done[half], None)

    out_ref[...] = dot(work[...], w_ref[...])


def own_joined_kernel(place, low_ref, high_ref, near_ref, w_ref, out_ref):
    for residue in range(4):
        lanes = [slice(head * HEAD_DIM, (head + 1) * HEAD_DIM) for head in range(residue, 2 * GROUP, 4)]
        rows = [
            jnp.concatenate([ref[c, :, at] for at in lanes], axis=1) for ref in (low_ref, high_ref) for c in range(2)
        ]
        term = dot(jnp.concatenate(rows, axis=0), jnp.concatenate([w_ref[at, :] for at in lanes], axis=0))
        for c in range(len(rows)):
            at = slice(c * CHUNK + residue * MID_ROWS, c * CHUNK + (residue + 1) * MID_ROWS)
            out_ref[at, :] = (near_ref[at, :] + term[c * MID_ROWS : (c + 1) * MID_ROWS]).astype(BF16)


def other_kernel(place, *refs):
    done, joined, own_ref, pieces = refs[0:2], refs[2], refs[3], list(refs[4:10])
    pieces += [jnp.concatenate([refs[n][...], refs[n + 1][...]], axis=0) for n in (10, 12)]
    out_ref, work = refs[-2:]
    me = place[0]

    @pl.when(pl.program_id(0) == 0)
    def _():
        assemble(work, done, joined)

    total = None
    for d in range(GROUP):
        at = pl.multiple_of((me ^ d) * 256, 256)
        term = dot(work[:, pl.ds(at, 256)], pieces[d][...])
        total = term if total is None else total + term
    mixed = (own_ref[...].astype(F32) + total.astype(BF16).astype(F32)).astype(BF16)
    row = token_of_row(iota((CHUNK, CHUNK), 1))
    pick = (row == iota((CHUNK, CHUNK), 0)).astype(F32).astype(BF16)
    for c in range(2):
        here = slice(c * CHUNK, (c + 1) * CHUNK)
        out_ref[here, :] = dot(pick, mixed[here]).astype(BF16)


def call(
    kernel,
    place,
    args,
    in_specs,
    out_specs,
    out_shape,
    grid,
    scratch=(),
    after=(),
    carry=(),
    into=(),
    flops=0,
    moved=0,
    name=None,
):
    count = len(args)
    outputs = len(out_shape)
    extra = len(after) + len(carry) + len(into)
    anywhere = pl.BlockSpec(memory_space=pl.ANY)

    def body(place_ref, *refs):
        results = refs[count + extra :]
        kernel(place_ref, *refs[:count], *results[:outputs], *results[outputs + len(carry) :])

    return pl.pallas_call(
        body,
        grid_spec=pltpu.PrefetchScalarGridSpec(
            num_scalar_prefetch=1,
            grid=grid,
            in_specs=list(in_specs) + [anywhere] * extra,
            out_specs=list(out_specs) + [anywhere] * len(carry),
            scratch_shapes=scratch,
        ),
        out_shape=list(out_shape) + [jax.ShapeDtypeStruct(a.shape, a.dtype) for a in carry],
        input_output_aliases={1 + count + len(after) + n: outputs + n for n in range(len(carry))}
        | {1 + count + len(after) + len(carry) + n: n for n in range(len(into))},
        compiler_params=pltpu.CompilerParams(vmem_limit_bytes=VMEM_BYTES),
        cost_estimate=pl.CostEstimate(flops=flops // COST_CUT, bytes_accessed=moved // COST_CUT, transcendentals=0),
        name=name,
    )(place, *args, *after, *carry, *into)


def fast_shards(queries, keys, values, out_weight):
    tokens, width = queries.shape
    heads = width // HEAD_DIM
    features = out_weight.shape[1]
    chunks = tokens // CHUNK
    mid_rows = tokens // 4
    far_rows = tokens // 16
    seq_size = lax.axis_size("seq")
    seq_index = lax.axis_index("seq")
    head_index = lax.axis_index("head")
    place = jnp.stack([seq_index % GROUP, seq_index // GROUP, head_index]).astype(jnp.int32)
    segments = [list(range(n, n + GROUP)) for n in range(0, seq_size, GROUP)]
    spec = pl.BlockSpec

    def array(*dims, kind=BF16):
        return jax.ShapeDtypeStruct(dims, kind)

    def whole(*dims):
        return spec(dims, lambda n, p: (0,) * len(dims))

    def exchange(blocks):
        return lax.all_to_all(blocks, "seq", 0, 0, axis_index_groups=segments, tiled=True)

    def over(distance, value):
        return lax.ppermute(value, "seq", [(i, i ^ distance) for i in range(seq_size)])

    def swapped(value):
        return lax.ppermute(value, "head", [(0, 1), (1, 0)])

    by_chunk = spec((CHUNK, width), lambda c, p: (c, 0))
    blocks_shape = (GROUP, 3 * chunks + 2, MID_ROWS, 256)
    far_shape = (GROUP, 2, far_rows, 256)
    blocks_sent, far = call(
        functools.partial(prep_kernel, chunks),
        place,
        (keys, values, queries),
        [by_chunk] * 3,
        [whole(*blocks_shape), whole(*far_shape)],
        [array(*blocks_shape), array(*far_shape)],
        (chunks,),
        flops=3 * 2 * tokens * 2 * MID_ROWS * width,
        moved=16 * 2**20,
        name="prep",
    )
    far = lax.ppermute(far, "seq", [(i, (i + GROUP) % seq_size) for i in range(seq_size)])
    out_half = features // 2
    piece_rows = width // GROUP
    piece = lax.dynamic_slice(
        out_weight, (seq_index % GROUP * piece_rows, (1 - head_index) * out_half), (piece_rows, out_half)
    )
    piece = swapped(piece)
    pairs = [(i, i + 1) for i in range(0, seq_size, 2)]
    prev_k = lax.ppermute(keys, "seq", pairs)
    prev_v = lax.ppermute(values, "seq", pairs)
    (ordered,) = call(
        reorder_kernel,
        place,
        (queries,),
        [by_chunk],
        [by_chunk],
        [array(tokens, width)],
        (chunks,),
        after=[blocks_sent],
        flops=2 * tokens * CHUNK * width,
        moved=8 * 2**20,
        name="reorder",
    )

    def near(part, first_head, after=()):
        head_count = heads // 2
        per_step = 4
        steps = head_count // per_step
        rows = tokens // 2
        wide = per_step * HEAD_DIM
        offset = first_head // per_step

        def columns(count, block):
            return spec((count, wide), lambda s, p: (block, offset + s))

        return call(
            functools.partial(near_kernel, part, per_step, first_head),
            place,
            (ordered, keys, values, prev_k, prev_v),
            [columns(rows, part)] + [columns(rows * (part + 1), 0)] * 2 + [columns(tokens, 0)] * 2,
            [
                spec((2, 3 * MID_ROWS, wide), lambda s, p: (0, 0, s)),
                spec((2, MID_ROWS, wide), lambda s, p: (0, 0, s)),
                whole(2, MID_ROWS, 128),
            ],
            [
                array(2, 3 * MID_ROWS, head_count * HEAD_DIM),
                array(2, MID_ROWS, head_count * HEAD_DIM),
                array(2, MID_ROWS, 128, kind=F32),
            ],
            (steps,),
            after=after,
            flops=4 * head_count * rows * (tokens + rows * (part + 1)) * HEAD_DIM,
            moved=2 * head_count * HEAD_DIM * (2 * rows + 4 * tokens),
            name="near",
        )

    parts = [near(0, 0)]
    got = [swapped(parts[0][0])]
    (blocks,) = call(
        fill_kernel,
        place,
        (far,),
        [whole(*far_shape)],
        [spec(far_shape, lambda n, p: (0, 3 * chunks // 2, 0, 0))],
        [array(*blocks_shape)],
        (1,),
        after=[parts[0][2], piece],
        into=[blocks_sent],
        name="fill",
    )
    parts.append(near(0, heads // 2, after=[blocks]))
    blocks = exchange(blocks)
    got.append(swapped(parts[1][0]))
    parts.append(near(1, 0, after=[parts[1][2]]))
    got.append(swapped(parts[2][0]))
    parts.append(near(1, heads // 2, after=[parts[2][2], got[0]]))
    got.append(swapped(parts[3][0]))
    (piece,) = call(gate_kernel, place, (), [], [], [], (1,), after=[parts[3][2], got[1]], carry=[piece], name="gate")
    pieces = {0: piece, 1: over(1, piece), 2: over(2, piece), 4: over(4, piece)}
    back_shape = (GROUP, mid_rows + STAT_ROWS, 256)
    (back,) = call(
        functools.partial(mid_kernel, chunks),
        place,
        (blocks,),
        [whole(*blocks_shape)],
        [whole(*back_shape)],
        [array(*back_shape)],
        (1,),
        scratch=[pltpu.VMEM((2, GROUP, mid_rows, 128), F32), pltpu.VMEM((2, GROUP, mid_rows, 128), F32)],
        after=[piece],
        flops=2 * 2 * (GROUP * mid_rows) ** 2 * HEAD_DIM,
        moved=6 * 2**20,
        name="mid",
    )
    done_shape = (2, 3 * MID_ROWS, width // 2)
    own_tile = 512
    own_tiles = out_half // own_tile
    own_block = spec((tokens, own_tile), lambda n, p: (0, n))
    own_weight = spec((width, own_tile), lambda n, p: (0, p[2] * own_tiles + n))
    (own_near,) = call(
        own_near_kernel,
        place,
        (*[part[0] for part in parts], out_weight),
        [whole(*done_shape)] * 4 + [own_weight],
        [own_block],
        [array(tokens, out_half, kind=F32)],
        (own_tiles,),
        scratch=[pltpu.VMEM((tokens, width), BF16)],
        after=[back],
        flops=2 * tokens * width * out_half,
        moved=2 * (width + 2 * tokens) * out_half,
        name="own_near",
    )
    (last_lse,) = call(
        gate_kernel,
        place,
        (),
        [],
        [],
        [],
        (1,),
        after=[own_near, got[2], pieces[2], pieces[4]],
        carry=[parts[3][2]],
        flops=2**46,
        name="gate",
    )
    parts[3] = [*parts[3][:2], last_lse]
    back = exchange(back)
    pieces[2], pieces[4] = call(
        gate_kernel, place, (), [], [], [], (1,), after=[back, last_lse], carry=[pieces[2], pieces[4]], name="gate"
    )
    half_piece = (piece_rows // 2, out_half)
    halves = call(
        halves_kernel,
        place,
        (pieces[2], pieces[4]),
        [spec(half_piece, lambda n, p: (0, 0)), spec(half_piece, lambda n, p: (1, 0))],
        [whole(*half_piece)] * 2,
        [array(*half_piece)] * 2,
        (1,),
        name="halves",
    )
    for d in (3, 5):
        pieces[d] = over(1, pieces[d ^ 1])
    corner = [over(4, halves[0]), over(2, halves[1])]
    joined_shape = (2, MID_ROWS, width)
    joined = call(
        functools.partial(combine_kernel, chunks),
        place,
        (*[part[1] for part in parts], *[part[2] for part in parts], back),
        [whole(2, MID_ROWS, width // 2)] * 4 + [whole(2, MID_ROWS, 128)] * 4 + [whole(*back_shape)],
        [whole(*joined_shape)] * 2,
        [array(*joined_shape)] * 2,
        (1,),
        flops=2**20,
        after=halves,
        moved=4 * 2**20,
        name="combine",
    )
    got_joined = [swapped(joined[0]), swapped(joined[1])]
    (own,) = call(
        own_joined_kernel,
        place,
        (*joined, own_near, out_weight),
        [whole(*joined_shape)] * 2 + [own_block, own_weight],
        [own_block],
        [array(tokens, out_half)],
        (own_tiles,),
        flops=2 * tokens * width * out_half // 4,
        moved=2 * (width + 3 * tokens) * out_half,
        name="own_joined",
    )
    corner = list(call(gate_kernel, place, (), [], [], [], (1,), after=[own, got[3]], carry=corner, name="gate"))
    corner += [over(1, half) for half in corner]
    tile = 1024
    rows = tokens // 2
    mixed = None
    for half in range(2):
        (mixed,) = call(
            other_kernel,
            place,
            (*got[2 * half : 2 * half + 2], got_joined[half], own, *[pieces[d] for d in range(GROUP - 2)], *corner),
            [whole(*done_shape)] * 2
            + [whole(*joined_shape), spec((rows, tile), lambda n, p, half=half: (half, n))]
            + [spec((piece_rows, tile), lambda n, p: (0, n))] * (GROUP - 2)
            + [spec((piece_rows // 2, tile), lambda n, p: (0, n))] * 4,
            [spec((rows, tile), lambda n, p, half=half: (half, n))],
            [array(tokens, out_half)],
            (out_half // tile,),
            scratch=[pltpu.VMEM((rows, width), BF16)],
            into=[] if mixed is None else [mixed],
            flops=2 * rows * width * out_half,
            moved=2 * width * out_half,
            name="other",
        )
    return mixed


def fits_fast(mesh, queries):
    seq, head = mesh.shape["seq"], mesh.shape["head"]
    tokens = queries.shape[0] // seq
    heads = queries.shape[1] // HEAD_DIM // head
    return (
        head == 2
        and heads == 2 * GROUP
        and seq == 2 * GROUP
        and tokens == 4 * CHUNK
        and SEG1 == 2 * tokens
        and SEG2 == GROUP * tokens
    )


def passed_along(value, axis, steps):
    count = lax.axis_size(axis)
    leading, last = (max(0, -steps), min(count, count - steps))
    return lax.ppermute(value, axis, [(source, source + steps) for source in range(leading, last)])


def attend_block(query, key_rows, value_rows, valid, scale):
    scores = jnp.einsum("qhd,khd->hqk", query, key_rows, preferred_element_type=jnp.float32) * scale
    scores = jnp.where(valid, scores, NEG_FILL)
    peak = jnp.max(scores, axis=-1)
    weights = jnp.where(valid, jnp.exp(scores - peak[..., None]), 0.0)
    total = jnp.sum(weights, axis=-1)
    numer = jnp.einsum(
        "hqk,khd->hqd", weights.astype(jnp.bfloat16), value_rows, preferred_element_type=jnp.float32
    )
    return (numer, peak, total)


def absorb_block(state, query, key_rows, value_rows, valid, scale):
    numer, peak, total = state
    scores = jnp.einsum("qhd,khd->hqk", query, key_rows, preferred_element_type=jnp.float32) * scale
    scores = jnp.where(valid, scores, NEG_FILL)
    new_peak = jnp.maximum(peak, jnp.max(scores, axis=-1))
    weights = jnp.where(valid, jnp.exp(scores - new_peak[..., None]), 0.0)
    added = jnp.einsum(
        "hqk,khd->hqd", weights.astype(jnp.bfloat16), value_rows, preferred_element_type=jnp.float32
    )
    return (added, new_peak, jnp.sum(weights, axis=-1))


def take_dilated(source, stride, offsets):
    count = source.shape[0] // stride
    shaped = source.reshape(count, stride, offsets.shape[0], -1)
    picker = (jnp.arange(stride)[:, None] == offsets[None, :]).astype(source.dtype)
    return jnp.sum(shaped * picker[None, :, :, None], axis=1).reshape(count, -1)


def spread_rows(state, stride, offsets):
    numer, peak, total = state
    heads_here, count = peak.shape
    picker = jnp.arange(stride)[None, :] == offsets[:, None]
    numer_full = jnp.where(picker[:, None, :, None], numer[:, :, None, :], 0.0).reshape(
        heads_here, count * stride, -1
    )
    peak_full = jnp.where(picker[:, None, :], peak[:, :, None], NEG_FILL).reshape(
        heads_here, count * stride
    )
    total_full = jnp.where(picker[:, None, :], total[:, :, None], 0.0).reshape(
        heads_here, count * stride
    )
    return (numer_full, peak_full, total_full)


def shards(queries, keys, values, out_weight):
    tok_rows = queries.shape[0]
    heads_here = queries.shape[1] // HEAD_DIM
    scale = 1.0 / math.sqrt(HEAD_DIM)
    seq_index = lax.axis_index("seq")
    head_index = lax.axis_index("head")
    head_ids = head_index * heads_here + jnp.arange(heads_here)
    query_pos = seq_index * tok_rows + jnp.arange(tok_rows)
    near_span = SEG1 // tok_rows
    near_keys, near_values = (keys, values)
    level_bit = 0
    moved = passed_along((near_keys, near_values), "seq", 1 << level_bit)
    near_keys = jnp.concatenate([moved[0], near_keys], axis=0)
    near_values = jnp.concatenate([moved[1], near_values], axis=0)
    near_pos = (seq_index - near_span + 1) * tok_rows + jnp.arange(near_span * tok_rows)
    near_start = seq_index // near_span * near_span * tok_rows
    near_valid = (near_pos[None, :] <= query_pos[:, None]) & (near_pos[None, :] >= near_start)

    def near_head(head_slot):
        column = head_slot * HEAD_DIM
        query = lax.dynamic_slice_in_dim(queries, column, HEAD_DIM, 1)[:, None, :]
        key_rows = lax.dynamic_slice_in_dim(near_keys, column, HEAD_DIM, 1)[:, None, :]
        value_rows = lax.dynamic_slice_in_dim(near_values, column, HEAD_DIM, 1)[:, None, :]
        numer, peak, total = attend_block(query, key_rows, value_rows, near_valid[None], scale)
        return (numer[0], peak[0], total[0])

    near_state = lax.map(near_head, jnp.arange(heads_here))
    mid_offsets = head_ids % 4
    far_offsets = head_ids % 16
    mid_count = tok_rows // 4
    far_count = tok_rows // 16
    mid_query = take_dilated(queries, 4, mid_offsets).reshape(mid_count, heads_here, HEAD_DIM)
    far_query = take_dilated(queries, 16, far_offsets).reshape(far_count, heads_here, HEAD_DIM)
    mid_keys = take_dilated(keys, 4, mid_offsets)
    mid_values = take_dilated(values, 4, mid_offsets)
    mid_qpos = seq_index * tok_rows + mid_offsets[:, None] + 4 * jnp.arange(mid_count)[None, :]
    far_qpos = seq_index * tok_rows + far_offsets[:, None] + 16 * jnp.arange(far_count)[None, :]
    mid_span = SEG2 // tok_rows
    mid_start = seq_index // mid_span * mid_span * tok_rows
    empty_far = (
        jnp.zeros((heads_here, far_count, HEAD_DIM), jnp.float32),
        jnp.full((heads_here, far_count), NEG_FILL, jnp.float32),
        jnp.zeros((heads_here, far_count), jnp.float32),
    )
    block_keys, block_values = (mid_keys, mid_values)
    for level_bit in range(mid_span.bit_length() - 1):
        moved = passed_along((block_keys, block_values), "seq", 1 << level_bit)
        block_keys = jnp.concatenate([moved[0], block_keys], axis=0)
        block_values = jnp.concatenate([moved[1], block_values], axis=0)
    key_index = jnp.arange(mid_span * mid_count)
    mid_kpos = (
        (seq_index - mid_span + 1) * tok_rows
        + (key_index // mid_count * tok_rows + 4 * (key_index % mid_count))[None, :]
        + mid_offsets[:, None]
    )
    mid_valid = (mid_kpos[:, None, :] <= mid_qpos[:, :, None]) & (mid_kpos[:, None, :] >= mid_start)
    mid_state = attend_block(
        mid_query,
        block_keys.reshape(-1, heads_here, HEAD_DIM),
        block_values.reshape(-1, heads_here, HEAD_DIM),
        mid_valid,
        scale,
    )
    far_keys = take_dilated(keys, 16, far_offsets)
    far_values = take_dilated(values, 16, far_offsets)
    piece = (
        lax.all_gather(far_keys, "seq", axis=0, tiled=True),
        lax.all_gather(far_values, "seq", axis=0, tiled=True),
    )
    count = piece[0].shape[0]
    row_index = jnp.arange(count)
    key_pos = (row_index // far_count * tok_rows + 16 * (row_index % far_count))[
        None, :
    ] + far_offsets[:, None]
    valid = key_pos[:, None, :] <= far_qpos[:, :, None]
    far_state = absorb_block(
        empty_far,
        far_query,
        piece[0].reshape(count, heads_here, HEAD_DIM),
        piece[1].reshape(count, heads_here, HEAD_DIM),
        valid,
        scale,
    )
    levels = (
        near_state,
        spread_rows(mid_state, 4, mid_offsets),
        spread_rows(far_state, 16, far_offsets),
    )
    top = jnp.maximum(jnp.maximum(levels[0][1], levels[1][1]), levels[2][1])
    numer = jnp.zeros_like(levels[0][0])
    total = jnp.zeros_like(levels[0][2])
    for level in levels:
        factor = jnp.exp(level[1] - top)
        numer = numer + level[0] * factor[..., None]
        total = total + level[2] * factor
    attended = (
        jnp.transpose(numer / total[..., None], (1, 0, 2))
        .reshape(tok_rows, -1)
        .astype(jnp.bfloat16)
    )
    terms = jnp.dot(attended, out_weight, preferred_element_type=jnp.float32)
    return lax.psum_scatter(terms.astype(jnp.bfloat16), "head", scatter_dimension=1, tiled=True)


def solution(mesh):
    placed = (P("seq", "head"), P("seq", "head"), P("seq", "head"), P("head", None))

    def whole(queries, keys, values, out_weight):
        body = fast_shards if fits_fast(mesh, queries) else shards
        mapped = jax.shard_map(body, mesh=mesh, in_specs=placed, out_specs=P("seq", "head"), check_vma=False)
        return mapped(queries, keys, values, out_weight)

    return whole
```

```python
import functools
import math

import jax
import jax.numpy as jnp
from jax import lax
from jax.experimental import pallas as pl
from jax.experimental.pallas import tpu as pltpu
from jax.sharding import PartitionSpec as P

HEAD_DIM = 128
SEG1 = 2048
SEG2 = 8192


NEG_FILL = -1e30
LOG2_SCALE = math.log2(math.e) / math.sqrt(HEAD_DIM)
CHUNK = 256
GROUP = 8
MID_ROWS = CHUNK // 4
FAR_ROWS = CHUNK // 16
STAT_ROWS = 16
VMEM_BYTES = 127 * 2**19
COST_CUT = 64
F32 = jnp.float32
BF16 = jnp.bfloat16


def iota(shape, dim):
    return lax.broadcasted_iota(jnp.int32, shape, dim)


def token_of_row(row):
    return 16 * (row & 15) + 4 * ((row >> 4) & 3) + (row >> 6)


def mid_of_row(row):
    return (row >> 6) * 64 + 4 * (row & 15) + ((row >> 4) & 3)


def dot(lhs, rhs):
    return lax.dot_general(lhs, rhs, (((1,), (0,)), ((), ())), preferred_element_type=F32)


def dot_t(lhs, rhs):
    return lax.dot_general(lhs, rhs, (((1,), (1,)), ((), ())), preferred_element_type=F32)


def with_ones(values):
    return jnp.concatenate([values, jnp.ones_like(values)], axis=1)


def attend_all(items):
    def scores(item):
        query = item[0]()
        found = []
        for keys, _, mask in item[1]():
            score = dot_t(query, keys())
            found.append(score if mask is None else jnp.where(mask, score, NEG_FILL))
        return found

    def weigh(found):
        peak = None
        for score in found:
            top = jnp.max(score, axis=1, keepdims=True)
            peak = top if peak is None else jnp.maximum(peak, top)
        return [jnp.exp2((score - peak) * LOG2_SCALE).astype(BF16) for score in found], peak

    def finish(item, weights, peak):
        acc = None
        for weight, (_, values, _) in zip(weights, item[1]()):
            term = dot(weight, with_ones(values()))
            acc = term if acc is None else acc + term
        total = acc[:, HEAD_DIM:]
        item[2](acc[:, :HEAD_DIM] / total, peak * LOG2_SCALE + jnp.log2(total))

    found = scores(items[0])
    waiting = None
    for n, item in enumerate(items):
        following = scores(items[n + 1]) if n + 1 < len(items) else None
        weights, peak = weigh(found)
        if waiting is not None:
            finish(*waiting)
        waiting = (item, weights, peak)
        found = following
    finish(*waiting)


def merge(out_a, lse_a, out_b, lse_b):
    top = jnp.maximum(lse_a, lse_b)
    fac_a = jnp.exp2(lse_a - top)
    fac_b = jnp.exp2(lse_b - top)
    total = fac_a + fac_b
    return (out_a * fac_a + out_b * fac_b) / total, top + jnp.log2(total)


def pick_rows(source, owner):
    row = iota((2 * MID_ROWS, CHUNK), 0)
    residue = 2 * (owner & 1) + (row >> 6)
    token = 16 * (row & 15) + 4 * ((row >> 4) & 3) + residue
    pick = (token == iota((2 * MID_ROWS, CHUNK), 1)).astype(F32).astype(BF16)
    both = dot(pick, source[:, owner * 256 : (owner + 1) * 256])
    return jnp.concatenate([both[:MID_ROWS, :128], both[MID_ROWS:, 128:]], axis=1).astype(BF16)


def prep_kernel(chunks, place, k_ref, v_ref, q_ref, w_ref, blocks_ref, far_ref, piece_ref):
    piece_ref[...] = w_ref[...]
    chunk = pl.program_id(0)
    at = pl.multiple_of(chunk * FAR_ROWS, FAR_ROWS)
    for owner in range(GROUP):
        start = ((owner >> 1) & 3) * FAR_ROWS
        for a, source in enumerate((k_ref, v_ref, q_ref)):
            rows = pick_rows(source, owner)
            blocks_ref[owner, a * chunks + chunk] = rows
            if a < 2:
                far_ref[owner, a, pl.ds(at, FAR_ROWS), :] = rows[start : start + FAR_ROWS]


def reorder_kernel(place, q_ref, rows_ref):
    row = iota((CHUNK, CHUNK), 0)
    pick = (token_of_row(row) == iota((CHUNK, CHUNK), 1)).astype(F32).astype(BF16)
    rows_ref[...] = dot(pick, q_ref[...]).astype(BF16)


def gate_kernel(place):
    pass


def fill_kernel(place, far_ref, blocks_ref):
    blocks_ref[...] = far_ref[...]


def near_kernel(part, per_step, first_head, place, q_ref, k_ref, v_ref, pk_ref, pv_ref, done_ref, kept_ref, lse_ref):
    step = pl.program_id(0)
    second = (place[0] & 1) == 1

    @pl.when(step == 0)
    def _():
        lse_ref[...] = jnp.zeros_like(lse_ref)

    token, column = token_of_row(iota((CHUNK, CHUNK), 0)), iota((CHUNK, CHUNK), 1)
    mask = token >= column

    def run(with_prev):
        items = []
        for e in range(per_step):
            lanes = slice(e * 128, (e + 1) * 128)
            for c in range(2):
                before = (2 * part + c) * CHUNK
                here = slice(c * CHUNK, (c + 1) * CHUNK)

                def query(here=here, lanes=lanes):
                    return q_ref[here, lanes]

                def pair(ref_k, ref_v, rows, mask, lanes=lanes):
                    return (lambda: ref_k[rows, lanes], lambda: ref_v[rows, lanes], mask)

                def parts(before=before, pair=pair):
                    found = [pair(k_ref, v_ref, slice(before, before + CHUNK), mask)]
                    if before:
                        found.append(pair(k_ref, v_ref, slice(0, before), None))
                    if with_prev:
                        found.append(pair(pk_ref, pv_ref, slice(None), None))
                    return found

                def store(out, lse, e=e, c=c, here=here, lanes=lanes):
                    residue = e % 4
                    out = out.astype(BF16)
                    for n, other in enumerate(r for r in range(4) if r != residue):
                        done_ref[c, n * MID_ROWS : (n + 1) * MID_ROWS, lanes] = out[
                            other * MID_ROWS : (other + 1) * MID_ROWS
                        ]
                    kept_ref[c, :, lanes] = out[residue * MID_ROWS : (residue + 1) * MID_ROWS]
                    kept = lse[residue * MID_ROWS : (residue + 1) * MID_ROWS]
                    head = first_head + step * per_step + e
                    lse_ref[c] = jnp.where(iota((MID_ROWS, 128), 1) == head, kept, lse_ref[c])

                items.append((query, parts, store))
        attend_all(items)

    @pl.when(second)
    def _():
        run(True)

    @pl.when(jnp.logical_not(second))
    def _():
        run(False)


def halves_kernel(rows, place, first_ref, second_ref, first_out, second_out, sems):
    copies = [
        pltpu.make_async_copy(first_ref.at[:rows], first_out, sems.at[0]),
        pltpu.make_async_copy(second_ref.at[rows:], second_out, sems.at[1]),
    ]
    for copy in copies:
        copy.start()
    for copy in copies:
        copy.wait()


def mid_kernel(chunks, place, blocks, out_ref, res, lses):
    me = place[0]
    segment = place[1]
    rows = chunks * MID_ROWS

    def taken(a, devices, lanes):
        return blocks[devices, a * chunks : (a + 1) * chunks, :, lanes].reshape(-1, 128)

    mask = mid_of_row(iota((rows, rows), 0)) >= mid_of_row(iota((rows, rows), 1))
    items = []
    for e in range(2):
        lanes = slice(e * 128, (e + 1) * 128)
        for i in range(GROUP):
            here, before = slice(i, i + 1), slice(0, i)

            def query(here=here, lanes=lanes):
                return taken(2, here, lanes)

            def parts(here=here, before=before, lanes=lanes):
                found = [(lambda: taken(0, here, lanes), lambda: taken(1, here, lanes), mask)]
                if before.stop:
                    found.append((lambda: taken(0, before, lanes), lambda: taken(1, before, lanes), None))
                return found

            def store(out, lse, e=e, i=i):
                res[e, i] = out
                lses[e, i] = lse

            items.append((query, parts, store))
    attend_all(items)

    start = pl.multiple_of(((me >> 1) & 3) * FAR_ROWS, FAR_ROWS)
    count = GROUP * chunks * FAR_ROWS
    mask = iota((count, count), 0) >= iota((count, count), 1)
    other_mask = jnp.broadcast_to(segment == 1, (count, count))
    items = []
    for e in range(2):
        lanes = slice(e * 128, (e + 1) * 128)

        def dilated(a, lanes=lanes):
            found = blocks[:, a * chunks : (a + 1) * chunks, pl.ds(start, FAR_ROWS), lanes]
            return found.reshape(count, 128)

        def other(a, lanes=lanes):
            return blocks[:, 3 * chunks + a, :, lanes].reshape(count, 128)

        def query(dilated=dilated):
            return dilated(2)

        def parts(dilated=dilated, other=other):
            return [
                (lambda: dilated(0), lambda: dilated(1), mask),
                (lambda: other(0), lambda: other(1), other_mask),
            ]

        def store(out, lse, e=e):
            for i in range(GROUP):
                for c in range(chunks):
                    at = pl.ds(start + c * MID_ROWS, FAR_ROWS)
                    first = (i * chunks + c) * FAR_ROWS
                    piece = slice(first, first + FAR_ROWS)
                    res[e, i, at, :], lses[e, i, at, :] = merge(
                        res[e, i, at, :], lses[e, i, at, :], out[piece], lse[piece]
                    )

        items.append((query, parts, store))
    attend_all(items)

    lane = iota((rows, 128), 1)
    stats = jnp.zeros((rows, 128), F32)
    for d in range(GROUP):
        for e in range(2):
            stats = jnp.where(lane == 8 * d + e, lses[e, d], stats)
            out_ref[d, :rows, e * 128 : (e + 1) * 128] = res[e, d].astype(BF16)
    stats = jnp.transpose(stats)
    high = stats.astype(BF16).astype(F32)
    low = stats - high
    for d in range(GROUP):
        out_ref[d, rows:, :] = jnp.concatenate([high[8 * d : 8 * d + 8], low[8 * d : 8 * d + 8]], axis=0).astype(BF16)


def locate(refs, column):
    for ref in refs:
        if column < ref.shape[-1]:
            return ref, column
        column -= ref.shape[-1]


def combine_kernel(chunks, place, *refs):
    kept, lses = refs[:4], refs[4:8]
    back, low_ref, high_ref = refs[8:]
    rows = chunks * MID_ROWS
    stats = []
    for d in range(GROUP):
        tile = back[d, rows:, :].astype(F32)
        stats.append((tile[:8] + tile[8:])[:2])
    stats.append(jnp.zeros((128 - 2 * GROUP, rows), F32))
    stats = jnp.transpose(jnp.concatenate(stats, axis=0))
    for c in range(chunks):
        first = c * MID_ROWS
        out_ref = low_ref if c < 2 else high_ref
        near_lse = lses[c // 2 * 2][c % 2] + lses[c // 2 * 2 + 1][c % 2]
        mid_lse = stats[first : first + MID_ROWS]
        top = jnp.maximum(near_lse, mid_lse)
        near_fac = jnp.exp2(near_lse - top)
        mid_fac = jnp.exp2(mid_lse - top)
        total = near_fac + mid_fac
        near_fac = near_fac / total
        mid_fac = mid_fac / total
        for d in range(GROUP):
            for e in range(2):
                column = d * 256 + e * 128
                head = 2 * d + e
                source, inner = locate(kept[c // 2 * 2 : c // 2 * 2 + 2], column)
                near = source[c % 2, :, inner : inner + 128].astype(F32)
                mid = back[d, first : first + MID_ROWS, e * 128 : (e + 1) * 128].astype(F32)
                out = near * near_fac[:, head : head + 1] + mid * mid_fac[:, head : head + 1]
                out_ref[c % 2, :, column : column + 128] = out.astype(BF16)


def assemble(work, done, joined):
    for head in range(2 * GROUP):
        residue = head % 4
        column = head * HEAD_DIM
        lanes = slice(column, column + HEAD_DIM)
        source, inner = locate(done, column)
        for c in range(2):
            for n, other in enumerate(r for r in range(4) if r != residue):
                at = slice(c * CHUNK + other * MID_ROWS, c * CHUNK + (other + 1) * MID_ROWS)
                work[at, lanes] = source[c, n * MID_ROWS : (n + 1) * MID_ROWS, inner : inner + HEAD_DIM]
            at = slice(c * CHUNK + residue * MID_ROWS, c * CHUNK + (residue + 1) * MID_ROWS)
            work[at, lanes] = jnp.zeros((MID_ROWS, HEAD_DIM), BF16) if joined is None else joined[c, :, lanes]


def own_near_kernel(place, *refs):
    done = refs[0:2], refs[2:4]
    w_ref, out_ref, work = refs[4:]

    @pl.when(pl.program_id(0) == 0)
    def _():
        for half in range(2):
            assemble(work.at[half * 2 * CHUNK : (half + 1) * 2 * CHUNK], done[half], None)

    out_ref[...] = dot(work[...], w_ref[...])


def own_joined_kernel(place, low_ref, high_ref, near_ref, w_ref, out_ref):
    for residue in range(4):
        lanes = [slice(head * HEAD_DIM, (head + 1) * HEAD_DIM) for head in range(residue, 2 * GROUP, 4)]
        rows = [
            jnp.concatenate([ref[c, :, at] for at in lanes], axis=1) for ref in (low_ref, high_ref) for c in range(2)
        ]
        term = dot(jnp.concatenate(rows, axis=0), jnp.concatenate([w_ref[at, :] for at in lanes], axis=0))
        for c in range(len(rows)):
            at = slice(c * CHUNK + residue * MID_ROWS, c * CHUNK + (residue + 1) * MID_ROWS)
            out_ref[at, :] = (near_ref[at, :] + term[c * MID_ROWS : (c + 1) * MID_ROWS]).astype(BF16)


def other_kernel(place, *refs):
    done, joined, own_ref, pieces = refs[0:2], refs[2], refs[3], refs[4:14]
    out_ref, work, weights = refs[14:]
    me = place[0]

    @pl.when(pl.program_id(0) == 0)
    def _():
        assemble(work, done, joined)

    for n, piece in enumerate(pieces):
        d, late = (n, 0) if n < GROUP - 2 else (GROUP - 2 + (n - GROUP + 2) // 2, n % 2)
        at = pl.multiple_of((me ^ d) * 256 + late * 128, 128)
        weights[pl.ds(at, piece.shape[0]), :] = piece[...]
    total = dot(work[...], weights[...])
    mixed = (own_ref[...].astype(F32) + total.astype(BF16).astype(F32)).astype(BF16)
    row = token_of_row(iota((CHUNK, CHUNK), 1))
    pick = (row == iota((CHUNK, CHUNK), 0)).astype(F32).astype(BF16)
    for c in range(2):
        here = slice(c * CHUNK, (c + 1) * CHUNK)
        out_ref[here, :] = dot(pick, mixed[here]).astype(BF16)


def call(
    kernel,
    place,
    args,
    in_specs,
    out_specs,
    out_shape,
    grid,
    scratch=(),
    after=(),
    carry=(),
    into=(),
    flops=0,
    moved=0,
    name=None,
):
    count = len(args)
    outputs = len(out_shape)
    extra = len(after) + len(carry) + len(into)
    anywhere = pl.BlockSpec(memory_space=pl.ANY)

    def body(place_ref, *refs):
        results = refs[count + extra :]
        kernel(place_ref, *refs[:count], *results[:outputs], *results[outputs + len(carry) :])

    return pl.pallas_call(
        body,
        grid_spec=pltpu.PrefetchScalarGridSpec(
            num_scalar_prefetch=1,
            grid=grid,
            in_specs=list(in_specs) + [anywhere] * extra,
            out_specs=list(out_specs) + [anywhere] * len(carry),
            scratch_shapes=scratch,
        ),
        out_shape=list(out_shape) + [jax.ShapeDtypeStruct(a.shape, a.dtype) for a in carry],
        input_output_aliases={1 + count + len(after) + n: outputs + n for n in range(len(carry))}
        | {1 + count + len(after) + len(carry) + n: n for n in range(len(into))},
        compiler_params=pltpu.CompilerParams(vmem_limit_bytes=VMEM_BYTES),
        cost_estimate=pl.CostEstimate(flops=flops // COST_CUT, bytes_accessed=moved // COST_CUT, transcendentals=0),
        name=name,
    )(place, *args, *after, *carry, *into)


def fast_shards(queries, keys, values, out_weight):
    tokens, width = queries.shape
    heads = width // HEAD_DIM
    features = out_weight.shape[1]
    chunks = tokens // CHUNK
    mid_rows = tokens // 4
    far_rows = tokens // 16
    seq_size = lax.axis_size("seq")
    seq_index = lax.axis_index("seq")
    head_index = lax.axis_index("head")
    place = jnp.stack([seq_index % GROUP, seq_index // GROUP, head_index]).astype(jnp.int32)
    segments = [list(range(n, n + GROUP)) for n in range(0, seq_size, GROUP)]
    spec = pl.BlockSpec
    anywhere = pl.BlockSpec(memory_space=pl.ANY)

    def array(*dims, kind=BF16):
        return jax.ShapeDtypeStruct(dims, kind)

    def whole(*dims):
        return spec(dims, lambda n, p: (0,) * len(dims))

    def exchange(blocks):
        return lax.all_to_all(blocks, "seq", 0, 0, axis_index_groups=segments, tiled=True)

    def over(distance, value):
        return lax.ppermute(value, "seq", [(i, i ^ distance) for i in range(seq_size)])

    def swapped(value):
        return lax.ppermute(value, "head", [(0, 1), (1, 0)])

    by_chunk = spec((CHUNK, width), lambda c, p: (c, 0))
    blocks_shape = (GROUP, 3 * chunks + 2, MID_ROWS, 256)
    far_shape = (GROUP, 2, far_rows, 256)
    out_half = features // 2
    piece_rows = width // GROUP
    piece_block = (piece_rows // chunks, out_half)
    blocks_sent, far, piece = call(
        functools.partial(prep_kernel, chunks),
        place,
        (keys, values, queries, out_weight),
        [by_chunk] * 3 + [spec(piece_block, lambda c, p: (p[0] * chunks + c, 1 - p[2]))],
        [whole(*blocks_shape), whole(*far_shape), spec(piece_block, lambda c, p: (c, 0))],
        [array(*blocks_shape), array(*far_shape), array(piece_rows, out_half)],
        (chunks,),
        flops=3 * 2 * tokens * 2 * MID_ROWS * width,
        moved=16 * 2**20,
        name="prep",
    )
    far = lax.ppermute(far, "seq", [(i, (i + GROUP) % seq_size) for i in range(seq_size)])
    piece = swapped(piece)
    pairs = [(i, i + 1) for i in range(0, seq_size, 2)]
    prev_k = lax.ppermute(keys, "seq", pairs)
    prev_v = lax.ppermute(values, "seq", pairs)
    (ordered,) = call(
        reorder_kernel,
        place,
        (queries,),
        [by_chunk],
        [by_chunk],
        [array(tokens, width)],
        (chunks,),
        after=[blocks_sent],
        flops=2 * tokens * CHUNK * width,
        moved=8 * 2**20,
        name="reorder",
    )

    def near(part, first_head, head_count, after=()):
        per_step = 4
        steps = head_count // per_step
        rows = tokens // 2
        wide = per_step * HEAD_DIM
        offset = first_head // per_step

        def columns(count, block):
            return spec((count, wide), lambda s, p: (block, offset + s))

        return call(
            functools.partial(near_kernel, part, per_step, first_head),
            place,
            (ordered, keys, values, prev_k, prev_v),
            [columns(rows, part)] + [columns(rows * (part + 1), 0)] * 2 + [columns(tokens, 0)] * 2,
            [
                spec((2, 3 * MID_ROWS, wide), lambda s, p: (0, 0, s)),
                spec((2, MID_ROWS, wide), lambda s, p: (0, 0, s)),
                whole(2, MID_ROWS, 128),
            ],
            [
                array(2, 3 * MID_ROWS, head_count * HEAD_DIM),
                array(2, MID_ROWS, head_count * HEAD_DIM),
                array(2, MID_ROWS, 128, kind=F32),
            ],
            (steps,),
            after=after,
            flops=4 * head_count * rows * (tokens + rows * (part + 1)) * HEAD_DIM,
            moved=2 * head_count * HEAD_DIM * (2 * rows + 4 * tokens),
            name="near",
        )

    first_heads = 3 * heads // 4
    parts = [near(0, 0, first_heads)]
    got = [swapped(parts[0][0])]
    (blocks,) = call(
        fill_kernel,
        place,
        (far,),
        [whole(*far_shape)],
        [spec(far_shape, lambda n, p: (0, 3 * chunks // 2, 0, 0))],
        [array(*blocks_shape)],
        (1,),
        after=[parts[0][2], piece],
        into=[blocks_sent],
        name="fill",
    )
    parts.append(near(0, first_heads, heads - first_heads, after=[blocks]))
    blocks = exchange(blocks)
    got.append(swapped(parts[1][0]))
    parts.append(near(1, 0, heads // 2, after=[parts[1][2]]))
    got.append(swapped(parts[2][0]))
    parts.append(near(1, heads // 2, heads // 2, after=[parts[2][2]]))
    got.append(swapped(parts[3][0]))
    (piece,) = call(gate_kernel, place, (), [], [], [], (1,), after=[parts[3][2], got[0], got[1]], carry=[piece], name="gate")
    pieces = {0: piece, 1: over(1, piece), 2: over(2, piece), 4: over(4, piece)}
    back_shape = (GROUP, mid_rows + STAT_ROWS, 256)
    (back,) = call(
        functools.partial(mid_kernel, chunks),
        place,
        (blocks,),
        [whole(*blocks_shape)],
        [whole(*back_shape)],
        [array(*back_shape)],
        (1,),
        scratch=[pltpu.VMEM((2, GROUP, mid_rows, 128), F32), pltpu.VMEM((2, GROUP, mid_rows, 128), F32)],
        after=[piece],
        flops=2 * 2 * (GROUP * mid_rows) ** 2 * HEAD_DIM,
        moved=6 * 2**20,
        name="mid",
    )
    own_tile = 512
    own_tiles = out_half // own_tile
    own_block = spec((tokens, own_tile), lambda n, p: (0, n))
    own_weight = spec((width, own_tile), lambda n, p: (0, p[2] * own_tiles + n))
    (own_near,) = call(
        own_near_kernel,
        place,
        (*[part[0] for part in parts], out_weight),
        [whole(*part[0].shape) for part in parts] + [own_weight],
        [own_block],
        [array(tokens, out_half, kind=F32)],
        (own_tiles,),
        scratch=[pltpu.VMEM((tokens, width), BF16)],
        after=[back],
        flops=2 * tokens * width * out_half,
        moved=2 * (width + 2 * tokens) * out_half,
        name="own_near",
    )
    (last_lse,) = call(
        gate_kernel,
        place,
        (),
        [],
        [],
        [],
        (1,),
        after=[own_near, got[2], pieces[2], pieces[4]],
        carry=[parts[3][2]],
        flops=2**46,
        name="gate",
    )
    parts[3] = [*parts[3][:2], last_lse]
    back = exchange(back)
    half_piece = array(piece_rows // 2, out_half)
    pieces[2], pieces[4], *halves = call(
        functools.partial(halves_kernel, piece_rows // 2),
        place,
        (),
        [],
        [anywhere] * 2 + [whole(*half_piece.shape)] * 2,
        [array(piece_rows, out_half)] * 2 + [half_piece] * 2,
        (1,),
        scratch=[pltpu.SemaphoreType.DMA((2,))],
        after=[back, last_lse, got[3]],
        into=[pieces[2], pieces[4]],
        name="halves",
    )
    for d in (3, 5):
        pieces[d] = over(1, pieces[d ^ 1])
    corner = [over(4, halves[0]), over(2, halves[1])]
    joined_shape = (2, MID_ROWS, width)
    joined = call(
        functools.partial(combine_kernel, chunks),
        place,
        (*[part[1] for part in parts], *[part[2] for part in parts], back),
        [whole(*part[1].shape) for part in parts] + [whole(2, MID_ROWS, 128)] * 4 + [whole(*back_shape)],
        [whole(*joined_shape)] * 2,
        [array(*joined_shape)] * 2,
        (1,),
        flops=2**20,
        after=halves,
        moved=4 * 2**20,
        name="combine",
    )
    got_joined = [swapped(joined[0]), swapped(joined[1])]
    (own,) = call(
        own_joined_kernel,
        place,
        (*joined, own_near, out_weight),
        [whole(*joined_shape)] * 2 + [own_block, own_weight],
        [own_block],
        [array(tokens, out_half)],
        (own_tiles,),
        after=[pieces[1], pieces[3], pieces[5]],
        flops=2 * tokens * width * out_half // 4,
        moved=2 * (width + 3 * tokens) * out_half,
        name="own_joined",
    )
    corner = list(call(gate_kernel, place, (), [], [], [], (1,), after=[own, got[3]], carry=corner, name="gate"))
    corner += [over(1, half) for half in corner]
    tile = 512
    rows = tokens // 2
    mixed = None
    for half in range(2):
        (mixed,) = call(
            other_kernel,
            place,
            (*got[2 * half : 2 * half + 2], got_joined[half], own, *[pieces[d] for d in range(GROUP - 2)], *corner),
            [whole(*done.shape) for done in got[2 * half : 2 * half + 2]]
            + [whole(*joined_shape), spec((rows, tile), lambda n, p, half=half: (half, n))]
            + [spec((piece_rows, tile), lambda n, p: (0, n))] * (GROUP - 2)
            + [spec((piece_rows // 2, tile), lambda n, p: (0, n))] * 4,
            [spec((rows, tile), lambda n, p, half=half: (half, n))],
            [array(tokens, out_half)],
            (out_half // tile,),
            scratch=[pltpu.VMEM((rows, width), BF16), pltpu.VMEM((width, tile), BF16)],
            into=[] if mixed is None else [mixed],
            flops=2 * rows * width * out_half,
            moved=2 * width * out_half,
            name="other",
        )
    return mixed


def fits_fast(mesh, queries):
    seq, head = mesh.shape["seq"], mesh.shape["head"]
    tokens = queries.shape[0] // seq
    heads = queries.shape[1] // HEAD_DIM // head
    return (
        head == 2
        and heads == 2 * GROUP
        and seq == 2 * GROUP
        and tokens == 4 * CHUNK
        and SEG1 == 2 * tokens
        and SEG2 == GROUP * tokens
    )


def passed_along(value, axis, steps):
    count = lax.axis_size(axis)
    leading, last = (max(0, -steps), min(count, count - steps))
    return lax.ppermute(value, axis, [(source, source + steps) for source in range(leading, last)])


def attend_block(query, key_rows, value_rows, valid, scale):
    scores = jnp.einsum("qhd,khd->hqk", query, key_rows, preferred_element_type=jnp.float32) * scale
    scores = jnp.where(valid, scores, NEG_FILL)
    peak = jnp.max(scores, axis=-1)
    weights = jnp.where(valid, jnp.exp(scores - peak[..., None]), 0.0)
    total = jnp.sum(weights, axis=-1)
    numer = jnp.einsum(
        "hqk,khd->hqd", weights.astype(jnp.bfloat16), value_rows, preferred_element_type=jnp.float32
    )
    return (numer, peak, total)


def absorb_block(state, query, key_rows, value_rows, valid, scale):
    numer, peak, total = state
    scores = jnp.einsum("qhd,khd->hqk", query, key_rows, preferred_element_type=jnp.float32) * scale
    scores = jnp.where(valid, scores, NEG_FILL)
    new_peak = jnp.maximum(peak, jnp.max(scores, axis=-1))
    weights = jnp.where(valid, jnp.exp(scores - new_peak[..., None]), 0.0)
    added = jnp.einsum(
        "hqk,khd->hqd", weights.astype(jnp.bfloat16), value_rows, preferred_element_type=jnp.float32
    )
    return (added, new_peak, jnp.sum(weights, axis=-1))


def take_dilated(source, stride, offsets):
    count = source.shape[0] // stride
    shaped = source.reshape(count, stride, offsets.shape[0], -1)
    picker = (jnp.arange(stride)[:, None] == offsets[None, :]).astype(source.dtype)
    return jnp.sum(shaped * picker[None, :, :, None], axis=1).reshape(count, -1)


def spread_rows(state, stride, offsets):
    numer, peak, total = state
    heads_here, count = peak.shape
    picker = jnp.arange(stride)[None, :] == offsets[:, None]
    numer_full = jnp.where(picker[:, None, :, None], numer[:, :, None, :], 0.0).reshape(
        heads_here, count * stride, -1
    )
    peak_full = jnp.where(picker[:, None, :], peak[:, :, None], NEG_FILL).reshape(
        heads_here, count * stride
    )
    total_full = jnp.where(picker[:, None, :], total[:, :, None], 0.0).reshape(
        heads_here, count * stride
    )
    return (numer_full, peak_full, total_full)


def shards(queries, keys, values, out_weight):
    tok_rows = queries.shape[0]
    heads_here = queries.shape[1] // HEAD_DIM
    scale = 1.0 / math.sqrt(HEAD_DIM)
    seq_index = lax.axis_index("seq")
    head_index = lax.axis_index("head")
    head_ids = head_index * heads_here + jnp.arange(heads_here)
    query_pos = seq_index * tok_rows + jnp.arange(tok_rows)
    near_span = SEG1 // tok_rows
    near_keys, near_values = (keys, values)
    level_bit = 0
    moved = passed_along((near_keys, near_values), "seq", 1 << level_bit)
    near_keys = jnp.concatenate([moved[0], near_keys], axis=0)
    near_values = jnp.concatenate([moved[1], near_values], axis=0)
    near_pos = (seq_index - near_span + 1) * tok_rows + jnp.arange(near_span * tok_rows)
    near_start = seq_index // near_span * near_span * tok_rows
    near_valid = (near_pos[None, :] <= query_pos[:, None]) & (near_pos[None, :] >= near_start)

    def near_head(head_slot):
        column = head_slot * HEAD_DIM
        query = lax.dynamic_slice_in_dim(queries, column, HEAD_DIM, 1)[:, None, :]
        key_rows = lax.dynamic_slice_in_dim(near_keys, column, HEAD_DIM, 1)[:, None, :]
        value_rows = lax.dynamic_slice_in_dim(near_values, column, HEAD_DIM, 1)[:, None, :]
        numer, peak, total = attend_block(query, key_rows, value_rows, near_valid[None], scale)
        return (numer[0], peak[0], total[0])

    near_state = lax.map(near_head, jnp.arange(heads_here))
    mid_offsets = head_ids % 4
    far_offsets = head_ids % 16
    mid_count = tok_rows // 4
    far_count = tok_rows // 16
    mid_query = take_dilated(queries, 4, mid_offsets).reshape(mid_count, heads_here, HEAD_DIM)
    far_query = take_dilated(queries, 16, far_offsets).reshape(far_count, heads_here, HEAD_DIM)
    mid_keys = take_dilated(keys, 4, mid_offsets)
    mid_values = take_dilated(values, 4, mid_offsets)
    mid_qpos = seq_index * tok_rows + mid_offsets[:, None] + 4 * jnp.arange(mid_count)[None, :]
    far_qpos = seq_index * tok_rows + far_offsets[:, None] + 16 * jnp.arange(far_count)[None, :]
    mid_span = SEG2 // tok_rows
    mid_start = seq_index // mid_span * mid_span * tok_rows
    empty_far = (
        jnp.zeros((heads_here, far_count, HEAD_DIM), jnp.float32),
        jnp.full((heads_here, far_count), NEG_FILL, jnp.float32),
        jnp.zeros((heads_here, far_count), jnp.float32),
    )
    block_keys, block_values = (mid_keys, mid_values)
    for level_bit in range(mid_span.bit_length() - 1):
        moved = passed_along((block_keys, block_values), "seq", 1 << level_bit)
        block_keys = jnp.concatenate([moved[0], block_keys], axis=0)
        block_values = jnp.concatenate([moved[1], block_values], axis=0)
    key_index = jnp.arange(mid_span * mid_count)
    mid_kpos = (
        (seq_index - mid_span + 1) * tok_rows
        + (key_index // mid_count * tok_rows + 4 * (key_index % mid_count))[None, :]
        + mid_offsets[:, None]
    )
    mid_valid = (mid_kpos[:, None, :] <= mid_qpos[:, :, None]) & (mid_kpos[:, None, :] >= mid_start)
    mid_state = attend_block(
        mid_query,
        block_keys.reshape(-1, heads_here, HEAD_DIM),
        block_values.reshape(-1, heads_here, HEAD_DIM),
        mid_valid,
        scale,
    )
    far_keys = take_dilated(keys, 16, far_offsets)
    far_values = take_dilated(values, 16, far_offsets)
    piece = (
        lax.all_gather(far_keys, "seq", axis=0, tiled=True),
        lax.all_gather(far_values, "seq", axis=0, tiled=True),
    )
    count = piece[0].shape[0]
    row_index = jnp.arange(count)
    key_pos = (row_index // far_count * tok_rows + 16 * (row_index % far_count))[
        None, :
    ] + far_offsets[:, None]
    valid = key_pos[:, None, :] <= far_qpos[:, :, None]
    far_state = absorb_block(
        empty_far,
        far_query,
        piece[0].reshape(count, heads_here, HEAD_DIM),
        piece[1].reshape(count, heads_here, HEAD_DIM),
        valid,
        scale,
    )
    levels = (
        near_state,
        spread_rows(mid_state, 4, mid_offsets),
        spread_rows(far_state, 16, far_offsets),
    )
    top = jnp.maximum(jnp.maximum(levels[0][1], levels[1][1]), levels[2][1])
    numer = jnp.zeros_like(levels[0][0])
    total = jnp.zeros_like(levels[0][2])
    for level in levels:
        factor = jnp.exp(level[1] - top)
        numer = numer + level[0] * factor[..., None]
        total = total + level[2] * factor
    attended = (
        jnp.transpose(numer / total[..., None], (1, 0, 2))
        .reshape(tok_rows, -1)
        .astype(jnp.bfloat16)
    )
    terms = jnp.dot(attended, out_weight, preferred_element_type=jnp.float32)
    return lax.psum_scatter(terms.astype(jnp.bfloat16), "head", scatter_dimension=1, tiled=True)


def solution(mesh):
    placed = (P("seq", "head"), P("seq", "head"), P("seq", "head"), P("head", None))

    def whole(queries, keys, values, out_weight):
        body = fast_shards if fits_fast(mesh, queries) else shards
        mapped = jax.shard_map(body, mesh=mesh, in_specs=placed, out_specs=P("seq", "head"), check_vma=False)
        return mapped(queries, keys, values, out_weight)

    return whole
```

```python
import functools
import math

import jax
import jax.numpy as jnp
from jax import lax
from jax.experimental import pallas as pl
from jax.experimental.pallas import tpu as pltpu
from jax.sharding import PartitionSpec as P

HEAD_DIM = 128
SEG1 = 2048
SEG2 = 8192


NEG_FILL = -1e30
LOG2_SCALE = math.log2(math.e) / math.sqrt(HEAD_DIM)
CHUNK = 256
GROUP = 8
MID_ROWS = CHUNK // 4
FAR_ROWS = CHUNK // 16
STAT_ROWS = 16
VMEM_BYTES = 127 * 2**19
COST_CUT = 64
F32 = jnp.float32
BF16 = jnp.bfloat16


def iota(shape, dim):
    return lax.broadcasted_iota(jnp.int32, shape, dim)


def token_of_row(row):
    return 16 * (row & 15) + 4 * ((row >> 4) & 3) + (row >> 6)


def mid_of_row(row):
    return (row >> 6) * 64 + 4 * (row & 15) + ((row >> 4) & 3)


def dot(lhs, rhs):
    return lax.dot_general(lhs, rhs, (((1,), (0,)), ((), ())), preferred_element_type=F32)


def dot_t(lhs, rhs):
    return lax.dot_general(lhs, rhs, (((1,), (1,)), ((), ())), preferred_element_type=F32)


def with_ones(values):
    return jnp.concatenate([values, jnp.ones_like(values)], axis=1)


def attend_all(items):
    def scores(item):
        query = item[0]()
        found = []
        for keys, _, mask in item[1]():
            score = dot_t(query, keys())
            found.append(score if mask is None else jnp.where(mask, score, NEG_FILL))
        return found

    def weigh(found):
        peak = None
        for score in found:
            top = jnp.max(score, axis=1, keepdims=True)
            peak = top if peak is None else jnp.maximum(peak, top)
        return [jnp.exp2((score - peak) * LOG2_SCALE).astype(BF16) for score in found], peak

    def finish(item, weights, peak):
        acc = None
        for weight, (_, values, _) in zip(weights, item[1]()):
            term = dot(weight, with_ones(values()))
            acc = term if acc is None else acc + term
        total = acc[:, HEAD_DIM:]
        item[2](acc[:, :HEAD_DIM] / total, peak * LOG2_SCALE + jnp.log2(total))

    found = scores(items[0])
    waiting = None
    for n, item in enumerate(items):
        following = scores(items[n + 1]) if n + 1 < len(items) else None
        weights, peak = weigh(found)
        if waiting is not None:
            finish(*waiting)
        waiting = (item, weights, peak)
        found = following
    finish(*waiting)


def merge(out_a, lse_a, out_b, lse_b):
    top = jnp.maximum(lse_a, lse_b)
    fac_a = jnp.exp2(lse_a - top)
    fac_b = jnp.exp2(lse_b - top)
    total = fac_a + fac_b
    return (out_a * fac_a + out_b * fac_b) / total, top + jnp.log2(total)


def pick_rows(source, owner):
    row = iota((2 * MID_ROWS, CHUNK), 0)
    residue = 2 * (owner & 1) + (row >> 6)
    token = 16 * (row & 15) + 4 * ((row >> 4) & 3) + residue
    pick = (token == iota((2 * MID_ROWS, CHUNK), 1)).astype(F32).astype(BF16)
    both = dot(pick, source[:, owner * 256 : (owner + 1) * 256])
    return jnp.concatenate([both[:MID_ROWS, :128], both[MID_ROWS:, 128:]], axis=1).astype(BF16)


def prep_kernel(chunks, place, k_ref, v_ref, q_ref, w_ref, blocks_ref, far_ref, piece_ref):
    piece_ref[...] = w_ref[...]
    chunk = pl.program_id(0)
    at = pl.multiple_of(chunk * FAR_ROWS, FAR_ROWS)
    for owner in range(GROUP):
        start = ((owner >> 1) & 3) * FAR_ROWS
        for a, source in enumerate((k_ref, v_ref, q_ref)):
            rows = pick_rows(source, owner)
            blocks_ref[owner, a * chunks + chunk] = rows
            if a < 2:
                far_ref[owner, a, pl.ds(at, FAR_ROWS), :] = rows[start : start + FAR_ROWS]


def reorder_kernel(place, q_ref, rows_ref):
    row = iota((CHUNK, CHUNK), 0)
    pick = (token_of_row(row) == iota((CHUNK, CHUNK), 1)).astype(F32).astype(BF16)
    rows_ref[...] = dot(pick, q_ref[...]).astype(BF16)


def gate_kernel(place):
    pass


def fill_kernel(place, far_ref, blocks_ref):
    blocks_ref[...] = far_ref[...]


def near_kernel(part, per_step, first_head, place, q_ref, k_ref, v_ref, pk_ref, pv_ref, done_ref, kept_ref, lse_ref):
    step = pl.program_id(0)
    second = (place[0] & 1) == 1

    @pl.when(step == 0)
    def _():
        lse_ref[...] = jnp.zeros_like(lse_ref)

    token, column = token_of_row(iota((CHUNK, CHUNK), 0)), iota((CHUNK, CHUNK), 1)
    mask = token >= column

    def run(with_prev):
        items = []
        for e in range(per_step):
            lanes = slice(e * 128, (e + 1) * 128)
            for c in range(2):
                before = (2 * part + c) * CHUNK
                here = slice(c * CHUNK, (c + 1) * CHUNK)

                def query(here=here, lanes=lanes):
                    return q_ref[here, lanes]

                def pair(ref_k, ref_v, rows, mask, lanes=lanes):
                    return (lambda: ref_k[rows, lanes], lambda: ref_v[rows, lanes], mask)

                def parts(before=before, pair=pair):
                    found = [pair(k_ref, v_ref, slice(before, before + CHUNK), mask)]
                    if before:
                        found.append(pair(k_ref, v_ref, slice(0, before), None))
                    if with_prev:
                        found.append(pair(pk_ref, pv_ref, slice(None), None))
                    return found

                def store(out, lse, e=e, c=c, here=here, lanes=lanes):
                    residue = e % 4
                    out = out.astype(BF16)
                    for n, other in enumerate(r for r in range(4) if r != residue):
                        done_ref[c, n * MID_ROWS : (n + 1) * MID_ROWS, lanes] = out[
                            other * MID_ROWS : (other + 1) * MID_ROWS
                        ]
                    kept_ref[c, :, lanes] = out[residue * MID_ROWS : (residue + 1) * MID_ROWS]
                    kept = lse[residue * MID_ROWS : (residue + 1) * MID_ROWS]
                    head = first_head + step * per_step + e
                    lse_ref[c] = jnp.where(iota((MID_ROWS, 128), 1) == head, kept, lse_ref[c])

                items.append((query, parts, store))
        attend_all(items)

    @pl.when(second)
    def _():
        run(True)

    @pl.when(jnp.logical_not(second))
    def _():
        run(False)


def halves_kernel(rows, place, first_ref, second_ref, first_out, second_out, sems):
    copies = [
        pltpu.make_async_copy(first_ref.at[:rows], first_out, sems.at[0]),
        pltpu.make_async_copy(second_ref.at[rows:], second_out, sems.at[1]),
    ]
    for copy in copies:
        copy.start()
    for copy in copies:
        copy.wait()


def mid_kernel(chunks, place, blocks, out_ref, res, lses):
    me = place[0]
    segment = place[1]
    rows = chunks * MID_ROWS

    def taken(a, devices, lanes):
        return blocks[devices, a * chunks : (a + 1) * chunks, :, lanes].reshape(-1, 128)

    mask = mid_of_row(iota((rows, rows), 0)) >= mid_of_row(iota((rows, rows), 1))
    items = []
    for e in range(2):
        lanes = slice(e * 128, (e + 1) * 128)
        for i in range(GROUP):
            here, before = slice(i, i + 1), slice(0, i)

            def query(here=here, lanes=lanes):
                return taken(2, here, lanes)

            def parts(here=here, before=before, lanes=lanes):
                found = [(lambda: taken(0, here, lanes), lambda: taken(1, here, lanes), mask)]
                if before.stop:
                    found.append((lambda: taken(0, before, lanes), lambda: taken(1, before, lanes), None))
                return found

            def store(out, lse, e=e, i=i):
                res[e, i] = out
                lses[e, i] = lse

            items.append((query, parts, store))
    attend_all(items)

    start = pl.multiple_of(((me >> 1) & 3) * FAR_ROWS, FAR_ROWS)
    count = GROUP * chunks * FAR_ROWS
    mask = iota((count, count), 0) >= iota((count, count), 1)
    other_mask = jnp.broadcast_to(segment == 1, (count, count))
    items = []
    for e in range(2):
        lanes = slice(e * 128, (e + 1) * 128)

        def dilated(a, lanes=lanes):
            found = blocks[:, a * chunks : (a + 1) * chunks, pl.ds(start, FAR_ROWS), lanes]
            return found.reshape(count, 128)

        def other(a, lanes=lanes):
            return blocks[:, 3 * chunks + a, :, lanes].reshape(count, 128)

        def query(dilated=dilated):
            return dilated(2)

        def parts(dilated=dilated, other=other):
            return [
                (lambda: dilated(0), lambda: dilated(1), mask),
                (lambda: other(0), lambda: other(1), other_mask),
            ]

        def store(out, lse, e=e):
            for i in range(GROUP):
                for c in range(chunks):
                    at = pl.ds(start + c * MID_ROWS, FAR_ROWS)
                    first = (i * chunks + c) * FAR_ROWS
                    piece = slice(first, first + FAR_ROWS)
                    res[e, i, at, :], lses[e, i, at, :] = merge(
                        res[e, i, at, :], lses[e, i, at, :], out[piece], lse[piece]
                    )

        items.append((query, parts, store))
    attend_all(items)

    lane = iota((rows, 128), 1)
    stats = jnp.zeros((rows, 128), F32)
    for d in range(GROUP):
        for e in range(2):
            stats = jnp.where(lane == 8 * d + e, lses[e, d], stats)
            out_ref[d, :rows, e * 128 : (e + 1) * 128] = res[e, d].astype(BF16)
    stats = jnp.transpose(stats)
    high = stats.astype(BF16).astype(F32)
    low = stats - high
    for d in range(GROUP):
        out_ref[d, rows:, :] = jnp.concatenate([high[8 * d : 8 * d + 8], low[8 * d : 8 * d + 8]], axis=0).astype(BF16)


def locate(refs, column):
    for ref in refs:
        if column < ref.shape[-1]:
            return ref, column
        column -= ref.shape[-1]


def combine_kernel(chunks, place, *refs):
    kept, lses = refs[:4], refs[4:8]
    back, low_ref, high_ref = refs[8:]
    rows = chunks * MID_ROWS
    stats = []
    for d in range(GROUP):
        tile = back[d, rows:, :].astype(F32)
        stats.append((tile[:8] + tile[8:])[:2])
    stats.append(jnp.zeros((128 - 2 * GROUP, rows), F32))
    stats = jnp.transpose(jnp.concatenate(stats, axis=0))
    for c in range(chunks):
        first = c * MID_ROWS
        out_ref = low_ref if c < 2 else high_ref
        near_lse = lses[c // 2 * 2][c % 2] + lses[c // 2 * 2 + 1][c % 2]
        mid_lse = stats[first : first + MID_ROWS]
        top = jnp.maximum(near_lse, mid_lse)
        near_fac = jnp.exp2(near_lse - top)
        mid_fac = jnp.exp2(mid_lse - top)
        total = near_fac + mid_fac
        near_fac = near_fac / total
        mid_fac = mid_fac / total
        for d in range(GROUP):
            for e in range(2):
                column = d * 256 + e * 128
                head = 2 * d + e
                source, inner = locate(kept[c // 2 * 2 : c // 2 * 2 + 2], column)
                near = source[c % 2, :, inner : inner + 128].astype(F32)
                mid = back[d, first : first + MID_ROWS, e * 128 : (e + 1) * 128].astype(F32)
                out = near * near_fac[:, head : head + 1] + mid * mid_fac[:, head : head + 1]
                out_ref[c % 2, :, column : column + 128] = out.astype(BF16)


def assemble(work, done, joined):
    for head in range(2 * GROUP):
        residue = head % 4
        column = head * HEAD_DIM
        lanes = slice(column, column + HEAD_DIM)
        source, inner = locate(done, column)
        for c in range(2):
            for n, other in enumerate(r for r in range(4) if r != residue):
                at = slice(c * CHUNK + other * MID_ROWS, c * CHUNK + (other + 1) * MID_ROWS)
                work[at, lanes] = source[c, n * MID_ROWS : (n + 1) * MID_ROWS, inner : inner + HEAD_DIM]
            at = slice(c * CHUNK + residue * MID_ROWS, c * CHUNK + (residue + 1) * MID_ROWS)
            work[at, lanes] = jnp.zeros((MID_ROWS, HEAD_DIM), BF16) if joined is None else joined[c, :, lanes]


def own_near_kernel(place, *refs):
    done = refs[0:2], refs[2:4]
    w_ref, out_ref, work = refs[4:]

    @pl.when(pl.program_id(0) == 0)
    def _():
        for half in range(2):
            assemble(work.at[half * 2 * CHUNK : (half + 1) * 2 * CHUNK], done[half], None)

    out_ref[...] = dot(work[...], w_ref[...])


def own_joined_kernel(place, low_ref, high_ref, near_ref, w_ref, out_ref):
    for residue in range(4):
        lanes = [slice(head * HEAD_DIM, (head + 1) * HEAD_DIM) for head in range(residue, 2 * GROUP, 4)]
        rows = [
            jnp.concatenate([ref[c, :, at] for at in lanes], axis=1) for ref in (low_ref, high_ref) for c in range(2)
        ]
        term = dot(jnp.concatenate(rows, axis=0), jnp.concatenate([w_ref[at, :] for at in lanes], axis=0))
        for c in range(len(rows)):
            at = slice(c * CHUNK + residue * MID_ROWS, c * CHUNK + (residue + 1) * MID_ROWS)
            out_ref[at, :] = (near_ref[at, :] + term[c * MID_ROWS : (c + 1) * MID_ROWS]).astype(BF16)


def other_kernel(place, *refs):
    done, joined, own_ref, pieces = refs[0:2], refs[2], refs[3], refs[4:14]
    out_ref, work, weights = refs[14:]
    me = place[0]

    @pl.when(pl.program_id(0) == 0)
    def _():
        assemble(work, done, joined)

    for n, piece in enumerate(pieces):
        d, late = (n, 0) if n < GROUP - 2 else (GROUP - 2 + (n - GROUP + 2) // 2, n % 2)
        at = pl.multiple_of((me ^ d) * 256 + late * 128, 128)
        weights[pl.ds(at, piece.shape[0]), :] = piece[...]
    total = dot(work[...], weights[...])
    mixed = (own_ref[...].astype(F32) + total.astype(BF16).astype(F32)).astype(BF16)
    row = token_of_row(iota((CHUNK, CHUNK), 1))
    pick = (row == iota((CHUNK, CHUNK), 0)).astype(F32).astype(BF16)
    for c in range(2):
        here = slice(c * CHUNK, (c + 1) * CHUNK)
        out_ref[here, :] = dot(pick, mixed[here]).astype(BF16)


def call(
    kernel,
    place,
    args,
    in_specs,
    out_specs,
    out_shape,
    grid,
    scratch=(),
    after=(),
    carry=(),
    into=(),
    flops=0,
    moved=0,
    name=None,
):
    count = len(args)
    outputs = len(out_shape)
    extra = len(after) + len(carry) + len(into)
    anywhere = pl.BlockSpec(memory_space=pl.ANY)

    def body(place_ref, *refs):
        results = refs[count + extra :]
        kernel(place_ref, *refs[:count], *results[:outputs], *results[outputs + len(carry) :])

    return pl.pallas_call(
        body,
        grid_spec=pltpu.PrefetchScalarGridSpec(
            num_scalar_prefetch=1,
            grid=grid,
            in_specs=list(in_specs) + [anywhere] * extra,
            out_specs=list(out_specs) + [anywhere] * len(carry),
            scratch_shapes=scratch,
        ),
        out_shape=list(out_shape) + [jax.ShapeDtypeStruct(a.shape, a.dtype) for a in carry],
        input_output_aliases={1 + count + len(after) + n: outputs + n for n in range(len(carry))}
        | {1 + count + len(after) + len(carry) + n: n for n in range(len(into))},
        compiler_params=pltpu.CompilerParams(vmem_limit_bytes=VMEM_BYTES),
        cost_estimate=pl.CostEstimate(flops=flops // COST_CUT, bytes_accessed=moved // COST_CUT, transcendentals=0),
        name=name,
    )(place, *args, *after, *carry, *into)


def fast_shards(queries, keys, values, out_weight):
    tokens, width = queries.shape
    heads = width // HEAD_DIM
    features = out_weight.shape[1]
    chunks = tokens // CHUNK
    mid_rows = tokens // 4
    far_rows = tokens // 16
    seq_size = lax.axis_size("seq")
    seq_index = lax.axis_index("seq")
    head_index = lax.axis_index("head")
    place = jnp.stack([seq_index % GROUP, seq_index // GROUP, head_index]).astype(jnp.int32)
    segments = [list(range(n, n + GROUP)) for n in range(0, seq_size, GROUP)]
    spec = pl.BlockSpec
    anywhere = pl.BlockSpec(memory_space=pl.ANY)

    def array(*dims, kind=BF16):
        return jax.ShapeDtypeStruct(dims, kind)

    def whole(*dims):
        return spec(dims, lambda n, p: (0,) * len(dims))

    def exchange(blocks):
        return lax.all_to_all(blocks, "seq", 0, 0, axis_index_groups=segments, tiled=True)

    def over(distance, value):
        return lax.ppermute(value, "seq", [(i, i ^ distance) for i in range(seq_size)])

    def swapped(value):
        return lax.ppermute(value, "head", [(0, 1), (1, 0)])

    by_chunk = spec((CHUNK, width), lambda c, p: (c, 0))
    blocks_shape = (GROUP, 3 * chunks + 2, MID_ROWS, 256)
    far_shape = (GROUP, 2, far_rows, 256)
    out_half = features // 2
    piece_rows = width // GROUP
    piece_block = (piece_rows // chunks, out_half)
    blocks_sent, far, piece = call(
        functools.partial(prep_kernel, chunks),
        place,
        (keys, values, queries, out_weight),
        [by_chunk] * 3 + [spec(piece_block, lambda c, p: (p[0] * chunks + c, 1 - p[2]))],
        [whole(*blocks_shape), whole(*far_shape), spec(piece_block, lambda c, p: (c, 0))],
        [array(*blocks_shape), array(*far_shape), array(piece_rows, out_half)],
        (chunks,),
        flops=3 * 2 * tokens * 2 * MID_ROWS * width,
        moved=16 * 2**20,
        name="prep",
    )
    far = lax.ppermute(far, "seq", [(i, (i + GROUP) % seq_size) for i in range(seq_size)])
    piece = swapped(piece)
    pairs = [(i, i + 1) for i in range(0, seq_size, 2)]
    prev_k = lax.ppermute(keys, "seq", pairs)
    prev_v = lax.ppermute(values, "seq", pairs)
    (ordered,) = call(
        reorder_kernel,
        place,
        (queries,),
        [by_chunk],
        [by_chunk],
        [array(tokens, width)],
        (chunks,),
        after=[blocks_sent],
        flops=2 * tokens * CHUNK * width,
        moved=8 * 2**20,
        name="reorder",
    )

    def near(part, first_head, head_count, after=()):
        per_step = 4
        steps = head_count // per_step
        rows = tokens // 2
        wide = per_step * HEAD_DIM
        offset = first_head // per_step

        def columns(count, block):
            return spec((count, wide), lambda s, p: (block, offset + s))

        return call(
            functools.partial(near_kernel, part, per_step, first_head),
            place,
            (ordered, keys, values, prev_k, prev_v),
            [columns(rows, part)] + [columns(rows * (part + 1), 0)] * 2 + [columns(tokens, 0)] * 2,
            [
                spec((2, 3 * MID_ROWS, wide), lambda s, p: (0, 0, s)),
                spec((2, MID_ROWS, wide), lambda s, p: (0, 0, s)),
                whole(2, MID_ROWS, 128),
            ],
            [
                array(2, 3 * MID_ROWS, head_count * HEAD_DIM),
                array(2, MID_ROWS, head_count * HEAD_DIM),
                array(2, MID_ROWS, 128, kind=F32),
            ],
            (steps,),
            after=after,
            flops=4 * head_count * rows * (tokens + rows * (part + 1)) * HEAD_DIM,
            moved=2 * head_count * HEAD_DIM * (2 * rows + 4 * tokens),
            name="near",
        )

    first_heads = 3 * heads // 4
    parts = [near(0, 0, first_heads)]
    got = [swapped(parts[0][0])]
    (blocks,) = call(
        fill_kernel,
        place,
        (far,),
        [whole(*far_shape)],
        [spec(far_shape, lambda n, p: (0, 3 * chunks // 2, 0, 0))],
        [array(*blocks_shape)],
        (1,),
        after=[parts[0][2], piece],
        into=[blocks_sent],
        name="fill",
    )
    parts.append(near(0, first_heads, heads - first_heads, after=[blocks]))
    blocks = exchange(blocks)
    got.append(swapped(parts[1][0]))
    parts.append(near(1, 0, heads // 2, after=[parts[1][2]]))
    got.append(swapped(parts[2][0]))
    parts.append(near(1, heads // 2, heads // 2, after=[parts[2][2]]))
    got.append(swapped(parts[3][0]))
    (piece,) = call(gate_kernel, place, (), [], [], [], (1,), after=[parts[3][2], got[0], got[1]], carry=[piece], name="gate")
    pieces = {0: piece, 1: over(1, piece), 2: over(2, piece), 4: over(4, piece)}
    back_shape = (GROUP, mid_rows + STAT_ROWS, 256)
    (back,) = call(
        functools.partial(mid_kernel, chunks),
        place,
        (blocks,),
        [whole(*blocks_shape)],
        [whole(*back_shape)],
        [array(*back_shape)],
        (1,),
        scratch=[pltpu.VMEM((2, GROUP, mid_rows, 128), F32), pltpu.VMEM((2, GROUP, mid_rows, 128), F32)],
        after=[piece],
        flops=2 * 2 * (GROUP * mid_rows) ** 2 * HEAD_DIM,
        moved=6 * 2**20,
        name="mid",
    )
    own_tile = 512
    own_tiles = out_half // own_tile
    own_block = spec((tokens, own_tile), lambda n, p: (0, n))
    own_weight = spec((width, own_tile), lambda n, p: (0, p[2] * own_tiles + n))
    (own_near,) = call(
        own_near_kernel,
        place,
        (*[part[0] for part in parts], out_weight),
        [whole(*part[0].shape) for part in parts] + [own_weight],
        [own_block],
        [array(tokens, out_half, kind=F32)],
        (own_tiles,),
        scratch=[pltpu.VMEM((tokens, width), BF16)],
        after=[back],
        flops=2 * tokens * width * out_half,
        moved=2 * (width + 2 * tokens) * out_half,
        name="own_near",
    )
    half_piece = array(piece_rows // 2, out_half)
    pieces[2], pieces[4], *halves, last_lse = call(
        functools.partial(halves_kernel, piece_rows // 2),
        place,
        (),
        [],
        [anywhere] * 2 + [whole(*half_piece.shape)] * 2,
        [array(piece_rows, out_half)] * 2 + [half_piece] * 2,
        (1,),
        scratch=[pltpu.SemaphoreType.DMA((2,))],
        after=[own_near, got[2]],
        carry=[parts[3][2]],
        into=[pieces[2], pieces[4]],
        flops=2**46,
        name="halves",
    )
    parts[3] = [*parts[3][:2], last_lse]
    back = exchange(back)
    pieces[2], pieces[4], *halves = call(
        gate_kernel,
        place,
        (),
        [],
        [],
        [],
        (1,),
        after=[back, last_lse, got[3]],
        carry=[pieces[2], pieces[4], *halves],
        name="gate",
    )
    for d in (3, 5):
        pieces[d] = over(1, pieces[d ^ 1])
    corner = [over(4, halves[0]), over(2, halves[1])]
    joined_shape = (2, MID_ROWS, width)
    joined = call(
        functools.partial(combine_kernel, chunks),
        place,
        (*[part[1] for part in parts], *[part[2] for part in parts], back),
        [whole(*part[1].shape) for part in parts] + [whole(2, MID_ROWS, 128)] * 4 + [whole(*back_shape)],
        [whole(*joined_shape)] * 2,
        [array(*joined_shape)] * 2,
        (1,),
        flops=2**20,
        after=halves,
        moved=4 * 2**20,
        name="combine",
    )
    got_joined = [swapped(joined[0]), swapped(joined[1])]
    (own,) = call(
        own_joined_kernel,
        place,
        (*joined, own_near, out_weight),
        [whole(*joined_shape)] * 2 + [own_block, own_weight],
        [own_block],
        [array(tokens, out_half)],
        (own_tiles,),
        after=[pieces[1], pieces[3], pieces[5]],
        flops=2 * tokens * width * out_half // 4,
        moved=2 * (width + 3 * tokens) * out_half,
        name="own_joined",
    )
    corner = list(call(gate_kernel, place, (), [], [], [], (1,), after=[own, got[3]], carry=corner, name="gate"))
    corner += [over(1, half) for half in corner]
    tile = 512
    rows = tokens // 2
    mixed = None
    for half in range(2):
        (mixed,) = call(
            other_kernel,
            place,
            (*got[2 * half : 2 * half + 2], got_joined[half], own, *[pieces[d] for d in range(GROUP - 2)], *corner),
            [whole(*done.shape) for done in got[2 * half : 2 * half + 2]]
            + [whole(*joined_shape), spec((rows, tile), lambda n, p, half=half: (half, n))]
            + [spec((piece_rows, tile), lambda n, p: (0, n))] * (GROUP - 2)
            + [spec((piece_rows // 2, tile), lambda n, p: (0, n))] * 4,
            [spec((rows, tile), lambda n, p, half=half: (half, n))],
            [array(tokens, out_half)],
            (out_half // tile,),
            scratch=[pltpu.VMEM((rows, width), BF16), pltpu.VMEM((width, tile), BF16)],
            into=[] if mixed is None else [mixed],
            flops=2 * rows * width * out_half,
            moved=2 * width * out_half,
            name="other",
        )
    return mixed


def fits_fast(mesh, queries):
    seq, head = mesh.shape["seq"], mesh.shape["head"]
    tokens = queries.shape[0] // seq
    heads = queries.shape[1] // HEAD_DIM // head
    return (
        head == 2
        and heads == 2 * GROUP
        and seq == 2 * GROUP
        and tokens == 4 * CHUNK
        and SEG1 == 2 * tokens
        and SEG2 == GROUP * tokens
    )


def passed_along(value, axis, steps):
    count = lax.axis_size(axis)
    leading, last = (max(0, -steps), min(count, count - steps))
    return lax.ppermute(value, axis, [(source, source + steps) for source in range(leading, last)])


def attend_block(query, key_rows, value_rows, valid, scale):
    scores = jnp.einsum("qhd,khd->hqk", query, key_rows, preferred_element_type=jnp.float32) * scale
    scores = jnp.where(valid, scores, NEG_FILL)
    peak = jnp.max(scores, axis=-1)
    weights = jnp.where(valid, jnp.exp(scores - peak[..., None]), 0.0)
    total = jnp.sum(weights, axis=-1)
    numer = jnp.einsum(
        "hqk,khd->hqd", weights.astype(jnp.bfloat16), value_rows, preferred_element_type=jnp.float32
    )
    return (numer, peak, total)


def absorb_block(state, query, key_rows, value_rows, valid, scale):
    numer, peak, total = state
    scores = jnp.einsum("qhd,khd->hqk", query, key_rows, preferred_element_type=jnp.float32) * scale
    scores = jnp.where(valid, scores, NEG_FILL)
    new_peak = jnp.maximum(peak, jnp.max(scores, axis=-1))
    weights = jnp.where(valid, jnp.exp(scores - new_peak[..., None]), 0.0)
    added = jnp.einsum(
        "hqk,khd->hqd", weights.astype(jnp.bfloat16), value_rows, preferred_element_type=jnp.float32
    )
    return (added, new_peak, jnp.sum(weights, axis=-1))


def take_dilated(source, stride, offsets):
    count = source.shape[0] // stride
    shaped = source.reshape(count, stride, offsets.shape[0], -1)
    picker = (jnp.arange(stride)[:, None] == offsets[None, :]).astype(source.dtype)
    return jnp.sum(shaped * picker[None, :, :, None], axis=1).reshape(count, -1)


def spread_rows(state, stride, offsets):
    numer, peak, total = state
    heads_here, count = peak.shape
    picker = jnp.arange(stride)[None, :] == offsets[:, None]
    numer_full = jnp.where(picker[:, None, :, None], numer[:, :, None, :], 0.0).reshape(
        heads_here, count * stride, -1
    )
    peak_full = jnp.where(picker[:, None, :], peak[:, :, None], NEG_FILL).reshape(
        heads_here, count * stride
    )
    total_full = jnp.where(picker[:, None, :], total[:, :, None], 0.0).reshape(
        heads_here, count * stride
    )
    return (numer_full, peak_full, total_full)


def shards(queries, keys, values, out_weight):
    tok_rows = queries.shape[0]
    heads_here = queries.shape[1] // HEAD_DIM
    scale = 1.0 / math.sqrt(HEAD_DIM)
    seq_index = lax.axis_index("seq")
    head_index = lax.axis_index("head")
    head_ids = head_index * heads_here + jnp.arange(heads_here)
    query_pos = seq_index * tok_rows + jnp.arange(tok_rows)
    near_span = SEG1 // tok_rows
    near_keys, near_values = (keys, values)
    level_bit = 0
    moved = passed_along((near_keys, near_values), "seq", 1 << level_bit)
    near_keys = jnp.concatenate([moved[0], near_keys], axis=0)
    near_values = jnp.concatenate([moved[1], near_values], axis=0)
    near_pos = (seq_index - near_span + 1) * tok_rows + jnp.arange(near_span * tok_rows)
    near_start = seq_index // near_span * near_span * tok_rows
    near_valid = (near_pos[None, :] <= query_pos[:, None]) & (near_pos[None, :] >= near_start)

    def near_head(head_slot):
        column = head_slot * HEAD_DIM
        query = lax.dynamic_slice_in_dim(queries, column, HEAD_DIM, 1)[:, None, :]
        key_rows = lax.dynamic_slice_in_dim(near_keys, column, HEAD_DIM, 1)[:, None, :]
        value_rows = lax.dynamic_slice_in_dim(near_values, column, HEAD_DIM, 1)[:, None, :]
        numer, peak, total = attend_block(query, key_rows, value_rows, near_valid[None], scale)
        return (numer[0], peak[0], total[0])

    near_state = lax.map(near_head, jnp.arange(heads_here))
    mid_offsets = head_ids % 4
    far_offsets = head_ids % 16
    mid_count = tok_rows // 4
    far_count = tok_rows // 16
    mid_query = take_dilated(queries, 4, mid_offsets).reshape(mid_count, heads_here, HEAD_DIM)
    far_query = take_dilated(queries, 16, far_offsets).reshape(far_count, heads_here, HEAD_DIM)
    mid_keys = take_dilated(keys, 4, mid_offsets)
    mid_values = take_dilated(values, 4, mid_offsets)
    mid_qpos = seq_index * tok_rows + mid_offsets[:, None] + 4 * jnp.arange(mid_count)[None, :]
    far_qpos = seq_index * tok_rows + far_offsets[:, None] + 16 * jnp.arange(far_count)[None, :]
    mid_span = SEG2 // tok_rows
    mid_start = seq_index // mid_span * mid_span * tok_rows
    empty_far = (
        jnp.zeros((heads_here, far_count, HEAD_DIM), jnp.float32),
        jnp.full((heads_here, far_count), NEG_FILL, jnp.float32),
        jnp.zeros((heads_here, far_count), jnp.float32),
    )
    block_keys, block_values = (mid_keys, mid_values)
    for level_bit in range(mid_span.bit_length() - 1):
        moved = passed_along((block_keys, block_values), "seq", 1 << level_bit)
        block_keys = jnp.concatenate([moved[0], block_keys], axis=0)
        block_values = jnp.concatenate([moved[1], block_values], axis=0)
    key_index = jnp.arange(mid_span * mid_count)
    mid_kpos = (
        (seq_index - mid_span + 1) * tok_rows
        + (key_index // mid_count * tok_rows + 4 * (key_index % mid_count))[None, :]
        + mid_offsets[:, None]
    )
    mid_valid = (mid_kpos[:, None, :] <= mid_qpos[:, :, None]) & (mid_kpos[:, None, :] >= mid_start)
    mid_state = attend_block(
        mid_query,
        block_keys.reshape(-1, heads_here, HEAD_DIM),
        block_values.reshape(-1, heads_here, HEAD_DIM),
        mid_valid,
        scale,
    )
    far_keys = take_dilated(keys, 16, far_offsets)
    far_values = take_dilated(values, 16, far_offsets)
    piece = (
        lax.all_gather(far_keys, "seq", axis=0, tiled=True),
        lax.all_gather(far_values, "seq", axis=0, tiled=True),
    )
    count = piece[0].shape[0]
    row_index = jnp.arange(count)
    key_pos = (row_index // far_count * tok_rows + 16 * (row_index % far_count))[
        None, :
    ] + far_offsets[:, None]
    valid = key_pos[:, None, :] <= far_qpos[:, :, None]
    far_state = absorb_block(
        empty_far,
        far_query,
        piece[0].reshape(count, heads_here, HEAD_DIM),
        piece[1].reshape(count, heads_here, HEAD_DIM),
        valid,
        scale,
    )
    levels = (
        near_state,
        spread_rows(mid_state, 4, mid_offsets),
        spread_rows(far_state, 16, far_offsets),
    )
    top = jnp.maximum(jnp.maximum(levels[0][1], levels[1][1]), levels[2][1])
    numer = jnp.zeros_like(levels[0][0])
    total = jnp.zeros_like(levels[0][2])
    for level in levels:
        factor = jnp.exp(level[1] - top)
        numer = numer + level[0] * factor[..., None]
        total = total + level[2] * factor
    attended = (
        jnp.transpose(numer / total[..., None], (1, 0, 2))
        .reshape(tok_rows, -1)
        .astype(jnp.bfloat16)
    )
    terms = jnp.dot(attended, out_weight, preferred_element_type=jnp.float32)
    return lax.psum_scatter(terms.astype(jnp.bfloat16), "head", scatter_dimension=1, tiled=True)


def solution(mesh):
    placed = (P("seq", "head"), P("seq", "head"), P("seq", "head"), P("head", None))

    def whole(queries, keys, values, out_weight):
        body = fast_shards if fits_fast(mesh, queries) else shards
        mapped = jax.shard_map(body, mesh=mesh, in_specs=placed, out_specs=P("seq", "head"), check_vma=False)
        return mapped(queries, keys, values, out_weight)

    return whole
```
